128 devices in a mesh: segment: 8 (over y, core), dp: 16 (over z, x).
Axes of the slice: x: 4, y: 4, z: 4, core: 2. Of those that a mesh axis runs over, the one named last changes fastest.
Arguments:
- tokens: bfloat16 [4096, 1280], P('dp'), may hold values from -6 to 6
- grad_out: bfloat16 [4096, 1280], P('dp'), may hold values from -6 to 6
- first_weight: bfloat16 [8, 1280, 1280], P('segment', 'dp'), may hold values from -0.15625 to 0.15625
- second_weight: bfloat16 [8, 1280, 1280], P('segment', 'dp'), may hold values from -0.15625 to 0.15625
- emb_table: float32 [1000, 1280], replicated, may hold values from -6 to 6
- level_scale: float32 [4, 1280], replicated, may hold values from 0.3 to 3
- timesteps: int32 [32], P('dp'), may hold values from 0 to 999
- levels: int32 [8], P('segment'), may hold values from 0 to 3
Outputs:
- first_grad: float32 [8, 1280, 1280], P('segment', 'dp')
- second_grad: float32 [8, 1280, 1280], P('segment', 'dp')
- input_grads: bfloat16 [8, 4096, 1280], P('segment', 'dp')
The draws below stay inside these ranges and needn't reach their ends.
All inputs are finite; a program needn't handle non-finite values.
Results may differ from the reference program's by a relative error of at most 0.025.
Values may be sent and summed in bfloat16 or wider, within the bound.
A program may use at most 64 MiB of HBM per device.

```python
import math
import jax
import jax.numpy as jnp
from jax import lax

C = 1280
STEPS = 1000
LEVELS = 4
SAMP_ROWS = 128
TOK_DEV = 256
SAMPLES = 32
TOKENS = 4096
N_SEGMENT = 8
N_DP = 16


def place_ends(values, own_key, low, top_value):
    extent = values.shape
    index_at = [jax.random.randint(jax.random.fold_in(own_key, axis), (), 0, extent[axis]) for axis in range(len(extent))]
    values = values.at[tuple(index_at)].set(low)
    longest = extent.index(max(extent))
    index_at[longest] = (index_at[longest] + 1) % extent[longest]
    return values.at[tuple(index_at)].set(top_value)


def level_of(own_key, shape, pieces, low, high):
    loudness, own = 1.0, jax.random.fold_in(own_key, 6)
    for axis_at, blocks in pieces:
        draws = jnp.exp(jax.random.uniform(jax.random.fold_in(own, axis_at), (blocks,), jnp.float32, low / len(pieces), high / len(pieces)))
        loudness = loudness * jnp.repeat(draws, shape[axis_at] // blocks).reshape([-1 if axis == axis_at else 1 for axis in range(len(shape))])
    return loudness


def bell_draw(key, dims, spread, most, split=(), dtype=jnp.bfloat16):
    values = spread * jax.random.normal(key, dims, jnp.float32)
    if split:
        values = values * level_of(key, dims, split, -0.22, 0.18)
    return jnp.clip(values, -most, most).astype(dtype)


def setup_inputs(seed: int = 0) -> dict:
    key_of = jax.random.split(jax.random.key(seed), 9)
    tokens = bell_draw(key_of[0], (TOKENS, C), 1.0, 6.0, ((0, 16),))
    grad_out = bell_draw(key_of[1], (TOKENS, C), 1.0, 6.0, ((0, 16),))
    first_weight = bell_draw(key_of[2], (N_SEGMENT, C, C), C ** -0.5, 0.15625, ((0, 8), (1, 16)))
    second_weight = bell_draw(key_of[3], (N_SEGMENT, C, C), C ** -0.5, 0.15625, ((0, 8), (1, 16)))
    emb_table = bell_draw(key_of[4], (STEPS, C), 1.0, 6.0, (), jnp.float32)
    level_scale = jnp.clip(jnp.exp(jax.random.uniform(key_of[5], (LEVELS, C), jnp.float32, math.log(0.3), math.log(3.0))), 0.3, 3.0)
    timesteps = place_ends(jax.random.randint(key_of[6], (SAMPLES,), 0, STEPS), jax.random.fold_in(key_of[6], 1), 0, STEPS - 1).astype(jnp.int32)
    levels = place_ends(jax.random.randint(key_of[7], (N_SEGMENT,), 0, LEVELS), jax.random.fold_in(key_of[7], 1), 0, LEVELS - 1).astype(jnp.int32)
    return dict(tokens=tokens, grad_out=grad_out, first_weight=first_weight, second_weight=second_weight, emb_table=emb_table, level_scale=level_scale, timesteps=timesteps, levels=levels)


epsilon = 1e-06

def normalize(values):
    return values * lax.rsqrt(lax.optimization_barrier(jnp.mean(values * values, axis=-1, keepdims=True)) + epsilon)

def silu_slope(preact):
    sigmoid_value = jax.nn.sigmoid(preact)
    return sigmoid_value * (1.0 + preact * (1.0 - sigmoid_value))

def group_sum(left, right):
    channels = left.shape[1]
    partial_terms = jnp.einsum('gti,gtj->gij', left.reshape(N_DP, TOK_DEV, channels).astype(jnp.float32), right.reshape(N_DP, TOK_DEV, channels).astype(jnp.float32))
    rounded = lax.optimization_barrier(partial_terms.astype(jnp.bfloat16))
    return lax.optimization_barrier(jnp.sum(rounded.astype(jnp.float32), axis=0))

def reference(tokens, grad_out, first_weight, second_weight, emb_table, level_scale, timesteps, levels):
    segment_count = N_SEGMENT
    mid_segment = segment_count // 2
    base_rows = jnp.repeat(emb_table[timesteps], SAMP_ROWS, axis=0)
    inputs, mixes, normeds, preacts, hiddens, outputs = ([], [], [], [], [], [])
    segment_input = tokens
    for segment in range(segment_count):
        if segment > mid_segment:
            segment_input = (segment_input.astype(jnp.float32) + outputs[segment_count - 1 - segment].astype(jnp.float32)).astype(jnp.bfloat16)
        mixed_input = segment_input.astype(jnp.float32) + base_rows * level_scale[levels[segment]][None, :]
        normed = normalize(mixed_input).astype(jnp.bfloat16)
        preact = jnp.dot(normed, first_weight[segment], preferred_element_type=jnp.float32)
        hidden = jax.nn.silu(preact).astype(jnp.bfloat16)
        result = (segment_input.astype(jnp.float32) + jnp.dot(hidden, second_weight[segment], preferred_element_type=jnp.float32)).astype(jnp.bfloat16)
        inputs.append(segment_input)
        mixes.append(mixed_input)
        normeds.append(normed)
        preacts.append(preact)
        hiddens.append(hidden)
        outputs.append(result)
        segment_input = result
    input_list = [None] * segment_count
    first_list = [None] * segment_count
    second_list = [None] * segment_count
    output_grad = grad_out
    for segment in range(segment_count - 1, -1, -1):
        if segment < segment_count - 1:
            output_grad = input_list[segment + 1]
            if segment < mid_segment - 1:
                output_grad = (output_grad.astype(jnp.float32) + input_list[segment_count - 1 - segment].astype(jnp.float32)).astype(jnp.bfloat16)
        hidden_grad = jnp.dot(output_grad, second_weight[segment].T, preferred_element_type=jnp.float32)
        preact_grad = (hidden_grad * silu_slope(preacts[segment])).astype(jnp.bfloat16)
        normed_grad = jnp.dot(preact_grad, first_weight[segment].T, preferred_element_type=jnp.float32)
        pullback = jax.vjp(normalize, mixes[segment])[1]
        mixed_grad = pullback(normed_grad)[0]
        input_list[segment] = (output_grad.astype(jnp.float32) + mixed_grad).astype(jnp.bfloat16)
        first_list[segment] = group_sum(normeds[segment], preact_grad)
        second_list[segment] = group_sum(hiddens[segment], output_grad)
    return (jnp.stack(first_list), jnp.stack(second_list), jnp.stack(input_list))
```

```python
import functools

import jax
import jax.numpy as jnp
from jax import lax
from jax.experimental import pallas as pl
from jax.experimental.pallas import tpu as pltpu
from jax.sharding import PartitionSpec as P

EPS = 1e-06
SECTIONS = 8
RING = 4
BLOCKS = 4
HALVES = ((0, 640), (640, 640))
F32 = jnp.float32
BF = jnp.bfloat16


def dot(a, b, contract):
    return lax.dot_general(a, b, (contract, ((), ())), preferred_element_type=F32)


def kernel(
    tok, go, w1, w2, emb, lvl, ts, lv,
    fg, sg, dxo,
    W1, W2, G1, G2, nT, hT,
    xr, sk, yb, nb, hb, un, sl, gr, gk, dz, dn, dx, rr, cond,
    embv, lvlv, acc1, acc2, r1, r2, r4, r5,
    gsend, grecv, ssend, srecv, psend, precv, lsem,
):
    seg = lax.axis_index("segment")
    dp = lax.axis_index("dp")
    z, x = dp // RING, dp % RING
    rows, chan = xr.shape
    step = rows // BLOCKS
    samples = ts.shape[0]

    def at_z(i):
        return lax.rem(z + i + RING, RING)

    def at_x(i):
        return lax.rem(x + i + RING, RING)

    def dev(axis, i):
        return {"dp": at_z(i) * RING + x} if axis == "z" else {"dp": z * RING + at_x(i)}

    own1 = pltpu.make_async_copy(w1.at[0], W1.at[z, x], lsem.at[0])
    own2 = pltpu.make_async_copy(w2.at[0], W2.at[z, x], lsem.at[1])
    table = pltpu.make_async_copy(emb, embv, lsem.at[2])
    scales = pltpu.make_async_copy(lvl, lvlv, lsem.at[3])
    own1.start()
    own2.start()
    table.start()
    scales.start()
    tok_in = pltpu.make_async_copy(tok, xr, lsem.at[4])
    go_in = pltpu.make_async_copy(go, gr, lsem.at[5])

    @pl.when(seg == 0)
    def _():
        tok_in.start()

    @pl.when(seg == SECTIONS - 1)
    def _():
        go_in.start()

    barrier = pltpu.get_barrier_semaphore()
    for axis in ("z", "x"):
        for way in (1, -1):
            pl.semaphore_signal(barrier, inc=1, device_id=dev(axis, way))

    @pl.when(seg > 0)
    def _():
        pl.semaphore_signal(barrier, inc=1, device_id={"segment": seg - 1})

    @pl.when(seg < SECTIONS - 1)
    def _():
        pl.semaphore_signal(barrier, inc=1, device_id={"segment": seg + 1})

    far = jnp.logical_or(seg < 3, seg > 4)

    @pl.when(far)
    def _():
        pl.semaphore_signal(barrier, inc=1, device_id={"segment": SECTIONS - 1 - seg})

    pl.semaphore_wait(
        barrier,
        4
        + (seg > 0).astype(jnp.int32)
        + (seg < SECTIONS - 1).astype(jnp.int32)
        + far.astype(jnp.int32),
    )
    own1.wait()
    own2.wait()

    units = [(w, h) for w in range(2) for h in range(2)]
    axes = (("x", "z"), ("z", "x"))
    offs = {"x": at_x, "z": at_z}

    def one(ref, h, first, second, part):
        i = (second, first) if h == 0 else (first, second)
        return ref.at[i[0], i[1], part, pl.ds(*HALVES[h])]

    def many(ref, h, second, part):
        if h == 0:
            return ref.at[second, part, :, pl.ds(*HALVES[h])]
        return ref.at[part, second, :, pl.ds(*HALVES[h])]

    ALL, TOP, LOW = pl.ds(0, 80), pl.ds(0, 48), pl.ds(48, 32)
    SUB, SUB0, SUB1 = pl.ds(0, 4), pl.ds(0, 2), pl.ds(2, 2)

    def gcopy(u, kind, ref, axis, way):
        k = u * 8 + kind
        return pltpu.make_async_remote_copy(
            src_ref=ref, dst_ref=ref, send_sem=gsend.at[k], recv_sem=grecv.at[k],
            device_id=dev(axis, way),
        )

    def gather_copy(u, kind):
        w, h = units[u]
        ref = (W1, W2)[w]
        a, b = axes[h]
        pa, pb = offs[a], offs[b]
        return (
            lambda: gcopy(u, 0, one(ref, h, pa(0), pb(0), ALL), a, 1),
            lambda: gcopy(u, 1, one(ref, h, pa(0), pb(0), ALL), a, -1),
            lambda: gcopy(u, 2, one(ref, h, pa(-1), pb(0), TOP), a, 1),
            lambda: gcopy(u, 3, one(ref, h, pa(1), pb(0), LOW), a, -1),
            lambda: gcopy(u, 4, many(ref, h, pb(0), SUB), b, 1),
            lambda: gcopy(u, 5, many(ref, h, pb(0), SUB), b, -1),
            lambda: gcopy(u, 6, many(ref, h, pb(-1), SUB0), b, 1),
            lambda: gcopy(u, 7, many(ref, h, pb(1), SUB1), b, -1),
        )[kind]()

    for u in range(4):
        gather_copy(u, 0).start()
        gather_copy(u, 1).start()
    for u in range(4):
        gather_copy(u, 0).wait_recv()
        gather_copy(u, 2).start()
        gather_copy(u, 1).wait_recv()
        gather_copy(u, 3).start()
    for u in range(4):
        gather_copy(u, 2).wait_recv()
        gather_copy(u, 3).wait_recv()
        gather_copy(u, 4).start()
        gather_copy(u, 5).start()
    for u in range(4):
        gather_copy(u, 4).wait_recv()
        gather_copy(u, 6).start()
        gather_copy(u, 5).wait_recv()
        gather_copy(u, 7).start()

    table.wait()
    scales.wait()
    scale_row = lvlv[pl.ds(lv[0], 1), :]
    for i in range(samples):
        cond[pl.ds(i, 1), :] = embv[pl.ds(ts[i], 1), :] * scale_row

    @pl.when(seg == 0)
    def _():
        tok_in.wait()

    @pl.when(seg == SECTIONS - 1)
    def _():
        go_in.wait()

    for u in range(4):
        gather_copy(u, 6).wait_recv()
        gather_copy(u, 7).wait_recv()

    def pcopy(kind, m, src, dst, to):
        k = kind * BLOCKS + m
        part = pl.ds(pl.multiple_of(m * step, step), step)
        return pltpu.make_async_remote_copy(
            src_ref=src.at[part, :], dst_ref=dst.at[part, :],
            send_sem=psend.at[k], recv_sem=precv.at[k], device_id={"segment": to},
        )

    def y_next(m):
        return pcopy(0, m, yb, xr, lax.rem(seg + 1, SECTIONS))

    def y_skip(m):
        return pcopy(1, m, yb, sk, SECTIONS - 1 - seg)

    def g_next(m):
        return pcopy(2, m, dx, gr, lax.rem(seg + SECTIONS - 1, SECTIONS))

    def g_skip(m):
        return pcopy(3, m, dx, gk, SECTIONS - 1 - seg)

    def forward(m, carry):
        part = pl.ds(pl.multiple_of(m * step, step), step)

        @pl.when(seg > 0)
        def _():
            y_next(m).wait_recv()

        @pl.when(seg > 4)
        def _():
            y_skip(m).wait_recv()
            xr[part, :] = (xr[part, :].astype(F32) + sk[part, :].astype(F32)).astype(BF)

        row = cond[pl.ds(m // (BLOCKS // samples), 1), :]
        u = xr[part, :].astype(F32) + row
        r = lax.rsqrt(jnp.mean(u * u, axis=-1, keepdims=True) + EPS)
        un[part, :] = u * r
        rr[part, :] = jnp.broadcast_to(r, (step, 128))
        n = (u * r).astype(BF)
        nb[part, :] = n
        for j in range(0, chan, 256):
            cols = pl.ds(j, 256)
            v = dot(n, W1[:, :, :, cols].reshape(chan, 256), ((1,), (0,)))
            s = jax.nn.sigmoid(v)
            hb[part, cols] = (v * s).astype(BF)
            sl[part, cols] = s * (1.0 + v * (1.0 - s))
        h = hb[part, :]
        for j in range(0, chan, 256):
            cols = pl.ds(j, 256)
            v = dot(h, W2[:, :, :, cols].reshape(chan, 256), ((1,), (0,)))
            yb[part, cols] = (xr[part, cols].astype(F32) + v).astype(BF)

        @pl.when(seg < SECTIONS - 1)
        def _():
            y_next(m).start()

        @pl.when(seg < 3)
        def _():
            y_skip(m).start()

        return carry

    lax.fori_loop(0, BLOCKS, forward, 0)

    def turn():
        nT[...] = nb[...].T.reshape(nT.shape)
        hT[...] = hb[...].T.reshape(hT.shape)

    @pl.when(seg < 6)
    def _():
        turn()

    def backward(m, carry):
        part = pl.ds(pl.multiple_of(m * step, step), step)

        @pl.when(seg < SECTIONS - 1)
        def _():
            g_next(m).wait_recv()

        @pl.when(seg < 3)
        def _():
            g_skip(m).wait_recv()
            gr[part, :] = (gr[part, :].astype(F32) + gk[part, :].astype(F32)).astype(BF)

        g = gr[part, :]
        for j in range(2):
            cols = pl.ds(640 * j, 640)
            v = dot(g, W2[2 * j : 2 * j + 2].reshape(640, chan), ((1,), (1,)))
            dz[part, cols] = (v * sl[part, cols]).astype(BF)
        d = dz[part, :]
        for j in range(2):
            cols = pl.ds(640 * j, 640)
            dn[:, cols] = dot(d, W1[2 * j : 2 * j + 2].reshape(640, chan), ((1,), (1,)))
        nrm = un[part, :]
        v = dn[...]
        along = jnp.mean(nrm * v, axis=-1, keepdims=True)
        r = rr[part, pl.ds(0, 1)]
        dx[part, :] = (g.astype(F32) + r * (v - nrm * along)).astype(BF)

        @pl.when(seg > 0)
        def _():
            g_next(m).start()

        @pl.when(seg > 4)
        def _():
            g_skip(m).start()

        return carry

    lax.fori_loop(0, BLOCKS, backward, 0)

    dx_out = pltpu.make_async_copy(dx, dxo.at[0], lsem.at[6])
    dx_out.start()

    @pl.when(seg >= 6)
    def _():
        turn()

    sunits = [(w, h) for w in (1, 0) for h in range(2)]

    def big(h, second, part):
        return (second, part) if h == 0 else (part, second)

    def product(u, second):
        w, h = sunits[u]
        left, right, to = ((nT, dz, G1), (hT, gr, G2))[w]
        i = big(h, second, slice(None))
        v = dot(left[i[0], i[1]].reshape(320, rows), right[:, pl.ds(*HALVES[h])], ((1,), (0,)))
        to[i[0], i[1], :, pl.ds(*HALVES[h])] = v.astype(BF).reshape(4, 80, 640)

    def scopy(u, kind, src, dst, axis, way):
        k = u * 8 + kind
        return pltpu.make_async_remote_copy(
            src_ref=src, dst_ref=dst, send_sem=ssend.at[k], recv_sem=srecv.at[k],
            device_id=dev(axis, way),
        )

    def scatter_copy(u, kind):
        w, h = sunits[u]
        ref = (G1, G2)[w]
        a, b = axes[h]
        pa, pb = offs[a], offs[b]
        return (
            lambda: scopy(u, 0, many(ref, h, pb(2), SUB0), r1.at[u, 0], b, 1),
            lambda: scopy(u, 1, many(ref, h, pb(2), SUB1), r1.at[u, 1], b, -1),
            lambda: scopy(u, 2, many(ref, h, pb(1), SUB), r2.at[u, 0], b, 1),
            lambda: scopy(u, 3, many(ref, h, pb(-1), SUB), r2.at[u, 1], b, -1),
            lambda: scopy(u, 4, one(ref, h, pa(2), pb(0), TOP), r4.at[u, pl.ds(0, 48)], a, 1),
            lambda: scopy(u, 5, one(ref, h, pa(2), pb(0), LOW), r4.at[u, pl.ds(48, 32)], a, -1),
            lambda: scopy(u, 6, one(ref, h, pa(1), pb(0), ALL), r5.at[u, 0], a, 1),
            lambda: scopy(u, 7, one(ref, h, pa(-1), pb(0), ALL), r5.at[u, 1], a, -1),
        )[kind]()

    def add(ref, *values):
        total = ref[...].astype(F32)
        for value in values:
            total = total + value.astype(F32)
        ref[...] = total.astype(BF)

    def parts(u):
        w, h = sunits[u]
        a, b = axes[h]
        return (G1, G2)[w], h, offs[a], offs[b]

    for u in range(4):
        ref, h, pa, pb = parts(u)
        product(u, pb(2))
        scatter_copy(u, 0).start()
        scatter_copy(u, 1).start()
    for u in range(4):
        ref, h, pa, pb = parts(u)
        product(u, pb(1))
        product(u, pb(-1))
        scatter_copy(u, 0).wait_recv()
        add(many(ref, h, pb(1), SUB0), r1[u, 0])
        scatter_copy(u, 2).start()
        scatter_copy(u, 1).wait_recv()
        add(many(ref, h, pb(-1), SUB1), r1[u, 1])
        scatter_copy(u, 3).start()
    for u in range(4):
        ref, h, pa, pb = parts(u)
        product(u, pb(0))
    for u in range(4):
        ref, h, pa, pb = parts(u)
        scatter_copy(u, 2).wait_recv()
        scatter_copy(u, 3).wait_recv()
        add(many(ref, h, pb(0), SUB), r2[u, 0], r2[u, 1])
        scatter_copy(u, 4).start()
        scatter_copy(u, 5).start()
    for u in range(4):
        ref, h, pa, pb = parts(u)
        scatter_copy(u, 4).wait_recv()
        add(one(ref, h, pa(1), pb(0), TOP), r4[u, pl.ds(0, 48)])
        scatter_copy(u, 6).start()
        scatter_copy(u, 5).wait_recv()
        add(one(ref, h, pa(-1), pb(0), LOW), r4[u, pl.ds(48, 32)])
        scatter_copy(u, 7).start()
    for u in range(4):
        w, h = sunits[u]
        ref, h, pa, pb = parts(u)
        scatter_copy(u, 6).wait_recv()
        scatter_copy(u, 7).wait_recv()
        total = one(ref, h, pa(0), pb(0), ALL)[...].astype(F32)
        total = total + r5[u, 0].astype(F32) + r5[u, 1].astype(F32)
        (acc1, acc2)[w][:, pl.ds(*HALVES[h])] = total
    out1 = pltpu.make_async_copy(acc1, fg.at[0], lsem.at[7])
    out2 = pltpu.make_async_copy(acc2, sg.at[0], lsem.at[8])
    out1.start()
    out2.start()

    for u in range(4):
        for kind in range(8):
            gather_copy(u, kind).wait_send()
            scatter_copy(u, kind).wait_send()

    def sent(m, carry):
        @pl.when(seg < SECTIONS - 1)
        def _():
            y_next(m).wait_send()

        @pl.when(seg < 3)
        def _():
            y_skip(m).wait_send()

        @pl.when(seg > 0)
        def _():
            g_next(m).wait_send()

        @pl.when(seg > 4)
        def _():
            g_skip(m).wait_send()

        return carry

    lax.fori_loop(0, BLOCKS, sent, 0)
    dx_out.wait()
    out1.wait()
    out2.wait()


def local(tokens, grad_out, first_weight, second_weight, emb_table, level_scale, timesteps, levels):
    rows, chan = tokens.shape
    depth = first_weight.shape[1]
    step = rows // BLOCKS
    samples = timesteps.shape[0]
    full = (RING, RING, depth, chan)
    vm = pltpu.VMEM
    dma = pltpu.SemaphoreType.DMA
    act = vm((rows, chan), BF)
    act32 = vm((rows, chan), F32)
    anyspec = pl.BlockSpec(memory_space=pl.ANY)
    smem = pl.BlockSpec(memory_space=pltpu.SMEM)
    macs = 6 * rows * chan * chan
    return pl.pallas_call(
        kernel,
        out_shape=(
            jax.ShapeDtypeStruct((1, depth, chan), F32),
            jax.ShapeDtypeStruct((1, depth, chan), F32),
            jax.ShapeDtypeStruct((1, rows, chan), BF),
        ),
        in_specs=[anyspec] * 6 + [smem] * 2,
        out_specs=(anyspec,) * 3,
        scratch_shapes=[
            vm(full, BF), vm(full, BF), vm(full, BF), vm(full, BF),
            vm((RING, RING, depth, rows), BF), vm((RING, RING, depth, rows), BF),
            act, act, act, act, act, act32, act32, act, act, act,
            vm((step, chan), F32), act, vm((rows, 128), F32), vm((samples, chan), F32),
            vm(emb_table.shape, F32), vm(level_scale.shape, F32),
            vm((depth, chan), F32), vm((depth, chan), F32),
            vm((4, 2, 2, depth, 640), BF), vm((4, 2, 4, depth, 640), BF),
            vm((4, depth, 640), BF), vm((4, 2, depth, 640), BF),
            dma((32,)), dma((32,)), dma((32,)), dma((32,)),
            dma((4 * BLOCKS,)), dma((4 * BLOCKS,)), dma((9,)),
        ],
        compiler_params=pltpu.CompilerParams(
            collective_id=0, has_side_effects=True, vmem_limit_bytes=60 * 1024 * 1024
        ),
        cost_estimate=pl.CostEstimate(
            flops=2 * macs, bytes_accessed=16 * 1024 * 1024, transcendentals=rows * chan
        ),
        name="sections",
    )(tokens, grad_out, first_weight, second_weight, emb_table, level_scale, timesteps, levels)


def solution(mesh):
    weights = P("segment", "dp", None)
    in_specs = (P("dp", None), P("dp", None), weights, weights, P(), P(), P("dp"), P("segment"))
    out_specs = (weights, weights, weights)
    return jax.shard_map(local, mesh=mesh, in_specs=in_specs, out_specs=out_specs, check_vma=False)
```

```python
import functools

import jax
import jax.numpy as jnp
from jax import lax
from jax.experimental import pallas as pl
from jax.experimental.pallas import tpu as pltpu
from jax.sharding import PartitionSpec as P

EPS = 1e-06
SECTIONS = 8
RING = 4
BLOCKS = 4
HALVES = ((0, 640), (640, 640))
F32 = jnp.float32
BF = jnp.bfloat16


def dot(a, b, contract):
    return lax.dot_general(a, b, (contract, ((), ())), preferred_element_type=F32)


def kernel(
    tok, go, w1, w2, emb, lvl, ts, lv,
    fg, sg, dxo,
    W1, W2, T1, T2, G1, G2, nT, hT,
    xr, sk, yb, nb, hb, un, sl, gr, gk, dz, dn, dx, rr, cond,
    embv, lvlv, acc1, acc2, r1, r2, r4, r5,
    gsend, grecv, ssend, srecv, psend, precv, lsem,
):
    seg = lax.axis_index("segment")
    dp = lax.axis_index("dp")
    z, x = dp // RING, dp % RING
    rows, chan = xr.shape
    step = rows // BLOCKS
    samples = ts.shape[0]

    def at_z(i):
        return lax.rem(z + i + RING, RING)

    def at_x(i):
        return lax.rem(x + i + RING, RING)

    def dev(axis, i):
        return {"dp": at_z(i) * RING + x} if axis == "z" else {"dp": z * RING + at_x(i)}

    own1 = pltpu.make_async_copy(w1.at[0], W1.at[z, x], lsem.at[0])
    own2 = pltpu.make_async_copy(w2.at[0], W2.at[z, x], lsem.at[1])
    table = pltpu.make_async_copy(emb, embv, lsem.at[2])
    scales = pltpu.make_async_copy(lvl, lvlv, lsem.at[3])
    own1.start()
    own2.start()
    table.start()
    scales.start()
    tok_in = pltpu.make_async_copy(tok, xr, lsem.at[4])
    go_in = pltpu.make_async_copy(go, gr, lsem.at[5])

    @pl.when(seg == 0)
    def _():
        tok_in.start()

    @pl.when(seg == SECTIONS - 1)
    def _():
        go_in.start()

    barrier = pltpu.get_barrier_semaphore()
    for axis in ("z", "x"):
        for way in (1, -1):
            pl.semaphore_signal(barrier, inc=1, device_id=dev(axis, way))

    @pl.when(seg > 0)
    def _():
        pl.semaphore_signal(barrier, inc=1, device_id={"segment": seg - 1})

    @pl.when(seg < SECTIONS - 1)
    def _():
        pl.semaphore_signal(barrier, inc=1, device_id={"segment": seg + 1})

    relay = jnp.logical_and(seg > 1, seg < 6)

    @pl.when(relay)
    def _():
        pl.semaphore_signal(barrier, inc=1, device_id={"segment": jnp.where(seg < 4, seg + 2, seg - 2)})

    far = jnp.logical_or(seg < 3, seg > 4)

    @pl.when(far)
    def _():
        pl.semaphore_signal(barrier, inc=1, device_id={"segment": SECTIONS - 1 - seg})

    pl.semaphore_wait(
        barrier,
        4
        + (seg > 0).astype(jnp.int32)
        + (seg < SECTIONS - 1).astype(jnp.int32)
        + far.astype(jnp.int32)
        + relay.astype(jnp.int32),
    )
    own1.wait()
    own2.wait()

    units = [(w, h) for w in range(2) for h in range(2)]
    axes = (("x", "z"), ("z", "x"))
    offs = {"x": at_x, "z": at_z}
    ALL, TOP, LOW = pl.ds(0, 80), pl.ds(0, 48), pl.ds(48, 32)

    def one(ref, h, first, second, part=ALL):
        i = (second, first) if h == 0 else (first, second)
        return ref.at[i[0], i[1], part, pl.ds(*HALVES[h])]

    def gcopy(u, kind, first, second, part, leg, way):
        w, h = units[u]
        ref = one((W1, W2)[w], h, offs[axes[h][0]](first), offs[axes[h][1]](second), part)
        k = u * 16 + kind
        return pltpu.make_async_remote_copy(
            src_ref=ref, dst_ref=ref, send_sem=gsend.at[k], recv_sem=grecv.at[k],
            device_id=dev(axes[h][leg], way),
        )

    NEAR = (0, -1, 1, 2)

    def first_leg(u, kind):
        return gcopy(
            u, kind, (0, 0, -1, 1)[kind], 0, (ALL, ALL, TOP, LOW)[kind], 0, (1, -1, 1, -1)[kind]
        )

    def second_leg(u, i, way):
        return gcopy(u, 4 + 2 * i + (way < 0), NEAR[i], 0, ALL, 1, way)

    def second_on(u, i):
        way = 1 if i < 2 else -1
        return gcopy(u, 12 + i, NEAR[i], -way, ALL, 1, way)

    def spread(u, i):
        second_leg(u, i, 1).start()
        second_leg(u, i, -1).start()

    def pass_on(u, i):
        second_leg(u, i, 1 if i < 2 else -1).wait_recv()
        second_on(u, i).start()

    for u in range(4):
        first_leg(u, 0).start()
        first_leg(u, 1).start()
    for u in range(4):
        spread(u, 0)
    for u in range(4):
        first_leg(u, 0).wait_recv()
        first_leg(u, 2).start()
        first_leg(u, 1).wait_recv()
        first_leg(u, 3).start()
        spread(u, 1)
        spread(u, 2)
    for u in range(4):
        pass_on(u, 0)
        first_leg(u, 2).wait_recv()
        first_leg(u, 3).wait_recv()
        spread(u, 3)
    for i in range(1, 4):
        for u in range(4):
            pass_on(u, i)

    table.wait()
    scales.wait()
    scale_row = lvlv[pl.ds(lv[0], 1), :]
    for i in range(samples):
        cond[pl.ds(i, 1), :] = embv[pl.ds(ts[i], 1), :] * scale_row

    @pl.when(seg == 0)
    def _():
        tok_in.wait()

    @pl.when(seg == SECTIONS - 1)
    def _():
        go_in.wait()

    for u in range(4):
        for i in range(4):
            second_leg(u, i, -1 if i < 2 else 1).wait_recv()
            second_on(u, i).wait_recv()

    def transpose_weights():
        for j in range(0, chan, 256):
            T1[pl.ds(j, 256), :] = W1[:, :, :, pl.ds(j, 256)].reshape(chan, 256).T
            T2[pl.ds(j, 256), :] = W2[:, :, :, pl.ds(j, 256)].reshape(chan, 256).T

    @pl.when(seg >= 4)
    def _():
        transpose_weights()

    def pcopy(kind, m, src, dst, to):
        k = kind * BLOCKS + m
        part = pl.ds(pl.multiple_of(m * step, step), step)
        return pltpu.make_async_remote_copy(
            src_ref=src.at[part, :], dst_ref=dst.at[part, :],
            send_sem=psend.at[k], recv_sem=precv.at[k], device_id={"segment": to},
        )

    def y_next(m):
        return pcopy(0, m, yb, xr, lax.rem(seg + 1, SECTIONS))

    def y_skip(m):
        return pcopy(1, m, yb, sk, SECTIONS - 1 - seg)

    def g_next(m):
        return pcopy(2, m, dx, gr, lax.rem(seg + SECTIONS - 1, SECTIONS))

    def g_skip(m):
        return pcopy(3, m, dx, gk, SECTIONS - 1 - seg)

    def y_relay(m):
        return pcopy(1, m, xr, sk, lax.rem(seg + 2, SECTIONS))

    def g_relay(m):
        return pcopy(3, m, gr, gk, lax.rem(seg + SECTIONS - 2, SECTIONS))

    early = BLOCKS // 2

    def y_direct(m):
        return jnp.logical_or(seg < 2, jnp.logical_and(seg == 2, m < early))

    def g_direct(m):
        return jnp.logical_or(seg > 5, jnp.logical_and(seg == 5, m < early))

    def forward(m, carry):
        part = pl.ds(pl.multiple_of(m * step, step), step)

        @pl.when(seg > 0)
        def _():
            y_next(m).wait_recv()

        @pl.when(seg > 4)
        def _():
            y_skip(m).wait_recv()
            xr[part, :] = (xr[part, :].astype(F32) + sk[part, :].astype(F32)).astype(BF)

        row = cond[pl.ds(m // (BLOCKS // samples), 1), :]
        u = xr[part, :].astype(F32) + row
        r = lax.rsqrt(jnp.mean(u * u, axis=-1, keepdims=True) + EPS)
        un[part, :] = u * r
        rr[part, :] = jnp.broadcast_to(r, (step, 128))
        n = (u * r).astype(BF)
        nb[part, :] = n
        for j in range(0, chan, 256):
            cols = pl.ds(j, 256)
            v = dot(n, W1[:, :, :, cols].reshape(chan, 256), ((1,), (0,)))
            s = jax.nn.sigmoid(v)
            hb[part, cols] = (v * s).astype(BF)
            sl[part, cols] = s * (1.0 + v * (1.0 - s))
        h = hb[part, :]
        for j in range(0, chan, 256):
            cols = pl.ds(j, 256)
            v = dot(h, W2[:, :, :, cols].reshape(chan, 256), ((1,), (0,)))
            yb[part, cols] = (xr[part, cols].astype(F32) + v).astype(BF)

        @pl.when(seg < SECTIONS - 1)
        def _():
            y_next(m).start()

        @pl.when(y_direct(m))
        def _():
            y_skip(m).start()

        return carry

    lax.fori_loop(0, BLOCKS, forward, 0)

    @pl.when(seg == 3)
    def _():
        for m in range(early, BLOCKS):
            y_relay(m).start()

    @pl.when(seg < 4)
    def _():
        transpose_weights()

    def turn():
        nT[...] = nb[...].T.reshape(nT.shape)
        hT[...] = hb[...].T.reshape(hT.shape)

    @pl.when(seg < 6)
    def _():
        turn()

    def backward(m, carry):
        part = pl.ds(pl.multiple_of(m * step, step), step)

        @pl.when(seg < SECTIONS - 1)
        def _():
            g_next(m).wait_recv()

        @pl.when(seg < 3)
        def _():
            g_skip(m).wait_recv()
            gr[part, :] = (gr[part, :].astype(F32) + gk[part, :].astype(F32)).astype(BF)

        g = gr[part, :]
        for j in range(0, chan, 256):
            cols = pl.ds(j, 256)
            v = dot(g, T2[:, cols], ((1,), (0,)))
            dz[part, cols] = (v * sl[part, cols]).astype(BF)
        d = dz[part, :]
        for j in range(0, chan, 256):
            cols = pl.ds(j, 256)
            dn[:, cols] = dot(d, T1[:, cols], ((1,), (0,)))
        nrm = un[part, :]
        v = dn[...]
        along = jnp.mean(nrm * v, axis=-1, keepdims=True)
        r = rr[part, pl.ds(0, 1)]
        dx[part, :] = (g.astype(F32) + r * (v - nrm * along)).astype(BF)

        @pl.when(seg > 0)
        def _():
            g_next(m).start()

        @pl.when(g_direct(m))
        def _():
            g_skip(m).start()

        return carry

    lax.fori_loop(0, BLOCKS, backward, 0)

    @pl.when(seg == 4)
    def _():
        for m in range(early, BLOCKS):
            g_relay(m).start()

    dx_out = pltpu.make_async_copy(dx, dxo.at[0], lsem.at[6])
    dx_out.start()

    @pl.when(seg >= 6)
    def _():
        turn()

    sunits = [(w, h) for w in (1, 0) for h in range(2)]
    FAR = (2, 1, -1, 0)

    def product(u, i):
        w, h = sunits[u]
        left, right, to = ((nT, dz, G1), (hT, gr, G2))[w]
        at = offs[axes[h][0]](FAR[i])
        at = (slice(None), at) if h == 0 else (at, slice(None))
        v = dot(left[at[0], at[1]].reshape(320, rows), right[:, pl.ds(*HALVES[h])], ((1,), (0,)))
        to[at[0], at[1], :, pl.ds(*HALVES[h])] = v.astype(BF).reshape(4, 80, 640)

    def block(u, first, second, part=ALL):
        w, h = sunits[u]
        return one((G1, G2)[w], h, offs[axes[h][0]](first), offs[axes[h][1]](second), part)

    def scopy(u, kind, src, dst, leg, way):
        k = u * 16 + kind
        return pltpu.make_async_remote_copy(
            src_ref=src, dst_ref=dst, send_sem=ssend.at[k], recv_sem=srecv.at[k],
            device_id=dev(axes[sunits[u][1]][leg], way),
        )

    def out_way(i):
        return 1 if i < 2 else -1

    def opposite(u, i):
        return scopy(u, i, block(u, FAR[i], 2), r1.at[u, i], 1, out_way(i))

    def beside(u, i, way):
        k = 4 + 2 * i + (way < 0)
        return scopy(u, k, block(u, FAR[i], way), r2.at[u, i, int(way < 0)], 1, way)

    def last_opposite(u, way):
        part = TOP if way > 0 else LOW
        return scopy(u, 12 + (way < 0), block(u, 2, 0, part), r4.at[u, part], 0, way)

    def last_beside(u, way):
        return scopy(u, 14 + (way < 0), block(u, way, 0), r5.at[u, int(way < 0)], 0, way)

    def add(ref, *values):
        total = ref[...].astype(F32)
        for value in values:
            total = total + value.astype(F32)
        ref[...] = total.astype(BF)

    def leave(u, i):
        product(u, i)
        opposite(u, i).start()

    def go_beside(u, i):
        way = out_way(i)
        beside(u, i, -way).start()
        opposite(u, i).wait_recv()
        add(block(u, FAR[i], way), r1[u, i])
        beside(u, i, way).start()

    def arrive(u, i):
        beside(u, i, 1).wait_recv()
        beside(u, i, -1).wait_recv()
        if i < 3:
            add(block(u, FAR[i], 0), r2[u, i, 0], r2[u, i, 1])
        if i == 0:
            last_opposite(u, 1).start()
            last_opposite(u, -1).start()
        elif i < 3:
            way = FAR[i]
            part = TOP if way > 0 else LOW
            last_opposite(u, way).wait_recv()
            add(block(u, way, 0, part), r4[u, part])
            last_beside(u, way).start()
        else:
            last_beside(u, 1).wait_recv()
            last_beside(u, -1).wait_recv()
            w, h = sunits[u]
            total = block(u, 0, 0)[...].astype(F32)
            for value in (r2[u, i, 0], r2[u, i, 1], r5[u, 0], r5[u, 1]):
                total = total + value.astype(F32)
            (acc1, acc2)[w][:, pl.ds(*HALVES[h])] = total

    for i in range(6):
        if i < 4:
            for u in range(4):
                leave(u, i)
        if 1 <= i < 5:
            for u in range(4):
                go_beside(u, i - 1)
        if 2 <= i:
            for u in range(4):
                arrive(u, i - 2)
    out1 = pltpu.make_async_copy(acc1, fg.at[0], lsem.at[7])
    out2 = pltpu.make_async_copy(acc2, sg.at[0], lsem.at[8])
    out1.start()
    out2.start()

    for u in range(4):
        for k in range(4):
            first_leg(u, k).wait_send()
            second_leg(u, k, 1).wait_send()
            second_leg(u, k, -1).wait_send()
            second_on(u, k).wait_send()
            opposite(u, k).wait_send()
            beside(u, k, 1).wait_send()
            beside(u, k, -1).wait_send()
        for way in (1, -1):
            last_opposite(u, way).wait_send()
            last_beside(u, way).wait_send()

    @pl.when(seg == 3)
    def _():
        for m in range(early, BLOCKS):
            y_relay(m).wait_send()

    @pl.when(seg == 4)
    def _():
        for m in range(early, BLOCKS):
            g_relay(m).wait_send()

    def sent(m, carry):
        @pl.when(seg < SECTIONS - 1)
        def _():
            y_next(m).wait_send()

        @pl.when(y_direct(m))
        def _():
            y_skip(m).wait_send()

        @pl.when(seg > 0)
        def _():
            g_next(m).wait_send()

        @pl.when(g_direct(m))
        def _():
            g_skip(m).wait_send()

        return carry

    lax.fori_loop(0, BLOCKS, sent, 0)
    dx_out.wait()
    out1.wait()
    out2.wait()


def local(tokens, grad_out, first_weight, second_weight, emb_table, level_scale, timesteps, levels):
    rows, chan = tokens.shape
    depth = first_weight.shape[1]
    step = rows // BLOCKS
    samples = timesteps.shape[0]
    full = (RING, RING, depth, chan)
    vm = pltpu.VMEM
    dma = pltpu.SemaphoreType.DMA
    act = vm((rows, chan), BF)
    act32 = vm((rows, chan), F32)
    anyspec = pl.BlockSpec(memory_space=pl.ANY)
    smem = pl.BlockSpec(memory_space=pltpu.SMEM)
    macs = 6 * rows * chan * chan
    return pl.pallas_call(
        kernel,
        out_shape=(
            jax.ShapeDtypeStruct((1, depth, chan), F32),
            jax.ShapeDtypeStruct((1, depth, chan), F32),
            jax.ShapeDtypeStruct((1, rows, chan), BF),
        ),
        in_specs=[anyspec] * 6 + [smem] * 2,
        out_specs=(anyspec,) * 3,
        scratch_shapes=[
            vm(full, BF), vm(full, BF), vm((chan, chan), BF), vm((chan, chan), BF),
            vm(full, BF), vm(full, BF),
            vm((RING, RING, depth, rows), BF), vm((RING, RING, depth, rows), BF),
            act, act, act, act, act, act32, act32, act, act, act,
            vm((step, chan), F32), act, vm((rows, 128), F32), vm((samples, chan), F32),
            vm(emb_table.shape, F32), vm(level_scale.shape, F32),
            vm((depth, chan), F32), vm((depth, chan), F32),
            vm((4, 4, depth, 640), BF), vm((4, 4, 2, depth, 640), BF),
            vm((4, depth, 640), BF), vm((4, 2, depth, 640), BF),
            dma((64,)), dma((64,)), dma((64,)), dma((64,)),
            dma((4 * BLOCKS,)), dma((4 * BLOCKS,)), dma((9,)),
        ],
        compiler_params=pltpu.CompilerParams(
            collective_id=0, has_side_effects=True, vmem_limit_bytes=60 * 1024 * 1024
        ),
        cost_estimate=pl.CostEstimate(
            flops=2 * macs, bytes_accessed=16 * 1024 * 1024, transcendentals=rows * chan
        ),
        name="sections",
    )(tokens, grad_out, first_weight, second_weight, emb_table, level_scale, timesteps, levels)


def solution(mesh):
    weights = P("segment", "dp", None)
    in_specs = (P("dp", None), P("dp", None), weights, weights, P(), P(), P("dp"), P("segment"))
    out_specs = (weights, weights, weights)
    return jax.shard_map(local, mesh=mesh, in_specs=in_specs, out_specs=out_specs, check_vma=False)
```

```python
import functools

import jax
import jax.numpy as jnp
from jax import lax
from jax.experimental import pallas as pl
from jax.experimental.pallas import tpu as pltpu
from jax.sharding import PartitionSpec as P

EPS = 1e-06
SECTIONS = 8
RING = 4
HELPER = 7
BLOCKS = 4
HALVES = ((0, 640), (640, 640))
F32 = jnp.float32
BF = jnp.bfloat16


def dot(a, b, contract):
    return lax.dot_general(a, b, (contract, ((), ())), preferred_element_type=F32)


def kernel(
    tok, go, w1, w2, emb, lvl, ts, lv,
    fg, sg, dxo,
    W1, W2, T1, T2, G1, G2, nT, hT,
    xr, sk, yb, nb, hb, un, sl, gr, gk, dz, dn, dx, rr, cond,
    hz, gz, hU, G3, accb, accr,
    embv, lvlv, acc1, acc2, r1, r2, r4, r5,
    gsend, grecv, ssend, srecv, psend, precv, lsem, turn_sem,
):
    seg = lax.axis_index("segment")
    dp = lax.axis_index("dp")
    z, x = dp // RING, dp % RING
    rows, chan = xr.shape
    step = rows // BLOCKS
    samples = ts.shape[0]

    def at_z(i):
        return lax.rem(z + i + RING, RING)

    def at_x(i):
        return lax.rem(x + i + RING, RING)

    def dev(axis, i):
        return {"dp": at_z(i) * RING + x} if axis == "z" else {"dp": z * RING + at_x(i)}

    own1 = pltpu.make_async_copy(w1.at[0], W1.at[z, x], lsem.at[0])
    own2 = pltpu.make_async_copy(w2.at[0], W2.at[z, x], lsem.at[1])
    table = pltpu.make_async_copy(emb, embv, lsem.at[2])
    scales = pltpu.make_async_copy(lvl, lvlv, lsem.at[3])
    own1.start()
    own2.start()
    table.start()
    scales.start()
    tok_in = pltpu.make_async_copy(tok, xr, lsem.at[4])
    go_in = pltpu.make_async_copy(go, gr, lsem.at[5])

    @pl.when(seg == 0)
    def _():
        tok_in.start()

    @pl.when(seg == SECTIONS - 1)
    def _():
        go_in.start()

    barrier = pltpu.get_barrier_semaphore()
    for axis in ("z", "x"):
        for way in (1, -1):
            pl.semaphore_signal(barrier, inc=1, device_id=dev(axis, way))

    @pl.when(seg > 0)
    def _():
        pl.semaphore_signal(barrier, inc=1, device_id={"segment": seg - 1})

    @pl.when(seg < SECTIONS - 1)
    def _():
        pl.semaphore_signal(barrier, inc=1, device_id={"segment": seg + 1})

    relay = jnp.logical_and(seg > 1, seg < 6)

    @pl.when(relay)
    def _():
        pl.semaphore_signal(barrier, inc=1, device_id={"segment": jnp.where(seg < 4, seg + 2, seg - 2)})

    far = jnp.logical_or(seg < 3, seg > 4)

    @pl.when(far)
    def _():
        pl.semaphore_signal(barrier, inc=1, device_id={"segment": SECTIONS - 1 - seg})

    pl.semaphore_wait(
        barrier,
        4
        + (seg > 0).astype(jnp.int32)
        + (seg < SECTIONS - 1).astype(jnp.int32)
        + far.astype(jnp.int32)
        + relay.astype(jnp.int32),
    )
    own1.wait()
    own2.wait()

    units = [(w, h) for w in range(2) for h in range(2)]
    axes = (("x", "z"), ("z", "x"))
    offs = {"x": at_x, "z": at_z}
    ALL, TOP, LOW = pl.ds(0, 80), pl.ds(0, 48), pl.ds(48, 32)

    def one(ref, h, first, second, part=ALL):
        i = (second, first) if h == 0 else (first, second)
        return ref.at[i[0], i[1], part, pl.ds(*HALVES[h])]

    def gcopy(u, kind, first, second, part, leg, way):
        w, h = units[u]
        ref = one((W1, W2)[w], h, offs[axes[h][0]](first), offs[axes[h][1]](second), part)
        k = u * 16 + kind
        return pltpu.make_async_remote_copy(
            src_ref=ref, dst_ref=ref, send_sem=gsend.at[k], recv_sem=grecv.at[k],
            device_id=dev(axes[h][leg], way),
        )

    NEAR = (0, -1, 1, 2)

    def first_leg(u, kind):
        return gcopy(
            u, kind, (0, 0, -1, 1)[kind], 0, (ALL, ALL, TOP, LOW)[kind], 0, (1, -1, 1, -1)[kind]
        )

    def second_leg(u, i, way):
        return gcopy(u, 4 + 2 * i + (way < 0), NEAR[i], 0, ALL, 1, way)

    def second_on(u, i):
        way = 1 if i < 2 else -1
        return gcopy(u, 12 + i, NEAR[i], -way, ALL, 1, way)

    def spread(u, i):
        second_leg(u, i, 1).start()
        second_leg(u, i, -1).start()

    def pass_on(u, i):
        second_leg(u, i, 1 if i < 2 else -1).wait_recv()
        second_on(u, i).start()

    odd = lax.rem(seg, 2) == 1

    @pl.when(odd)
    def _():
        pl.semaphore_wait(turn_sem, 1)

    for u in range(4):
        first_leg(u, 0).start()
        first_leg(u, 1).start()
    for u in range(4):
        spread(u, 0)
    for u in range(4):
        first_leg(u, 0).wait_recv()
        first_leg(u, 2).start()
        first_leg(u, 1).wait_recv()
        first_leg(u, 3).start()
        spread(u, 1)
        spread(u, 2)
    for u in range(4):
        pass_on(u, 0)
        first_leg(u, 2).wait_recv()
        first_leg(u, 3).wait_recv()
        spread(u, 3)

    @pl.when(jnp.logical_not(odd))
    def _():
        pl.semaphore_signal(turn_sem, inc=1, device_id={"segment": lax.rem(seg + 1, SECTIONS)})

    for i in range(1, 4):
        for u in range(4):
            pass_on(u, i)

    table.wait()
    scales.wait()
    scale_row = lvlv[pl.ds(lv[0], 1), :]
    for i in range(samples):
        cond[pl.ds(i, 1), :] = embv[pl.ds(ts[i], 1), :] * scale_row

    @pl.when(seg == 0)
    def _():
        tok_in.wait()

    @pl.when(seg == SECTIONS - 1)
    def _():
        go_in.wait()

    for u in range(4):
        for i in range(4):
            second_leg(u, i, -1 if i < 2 else 1).wait_recv()
            second_on(u, i).wait_recv()

    def transpose_weights():
        for j in range(0, chan, 256):
            T1[pl.ds(j, 256), :] = W1[:, :, :, pl.ds(j, 256)].reshape(chan, 256).T
            T2[pl.ds(j, 256), :] = W2[:, :, :, pl.ds(j, 256)].reshape(chan, 256).T

    @pl.when(seg >= 4)
    def _():
        transpose_weights()

    def pcopy(kind, m, src, dst, to):
        k = kind * BLOCKS + m
        part = pl.ds(pl.multiple_of(m * step, step), step)
        return pltpu.make_async_remote_copy(
            src_ref=src.at[part, :], dst_ref=dst.at[part, :],
            send_sem=psend.at[k], recv_sem=precv.at[k], device_id={"segment": to},
        )

    def y_next(m):
        return pcopy(0, m, yb, xr, lax.rem(seg + 1, SECTIONS))

    def y_skip(m):
        return pcopy(1, m, yb, sk, SECTIONS - 1 - seg)

    def g_next(m):
        return pcopy(2, m, dx, gr, lax.rem(seg + SECTIONS - 1, SECTIONS))

    def g_skip(m):
        return pcopy(3, m, dx, gk, SECTIONS - 1 - seg)

    def y_relay(m):
        return pcopy(1, m, xr, sk, lax.rem(seg + 2, SECTIONS))

    def g_relay(m):
        return pcopy(3, m, gr, gk, lax.rem(seg + SECTIONS - 2, SECTIONS))

    def h_out(m):
        return pcopy(4, m, hb, hz, HELPER)

    def g_out(m):
        return pcopy(5, m, gr, gz, HELPER)

    early = BLOCKS // 2

    def y_direct(m):
        return jnp.logical_or(seg < 2, jnp.logical_and(seg == 2, m < early))

    def g_direct(m):
        return jnp.logical_or(seg > 5, jnp.logical_and(seg == 5, m < early))

    def forward(m, carry):
        part = pl.ds(pl.multiple_of(m * step, step), step)

        @pl.when(seg > 0)
        def _():
            y_next(m).wait_recv()

        @pl.when(seg > 4)
        def _():
            y_skip(m).wait_recv()
            xr[part, :] = (xr[part, :].astype(F32) + sk[part, :].astype(F32)).astype(BF)

        row = cond[pl.ds(m // (BLOCKS // samples), 1), :]
        u = xr[part, :].astype(F32) + row
        r = lax.rsqrt(jnp.mean(u * u, axis=-1, keepdims=True) + EPS)
        un[part, :] = u * r
        rr[part, :] = jnp.broadcast_to(r, (step, 128))
        n = (u * r).astype(BF)
        nb[part, :] = n
        for j in range(0, chan, 256):
            cols = pl.ds(j, 256)
            v = dot(n, W1[:, :, :, cols].reshape(chan, 256), ((1,), (0,)))
            s = jax.nn.sigmoid(v)
            hb[part, cols] = (v * s).astype(BF)
            sl[part, cols] = s * (1.0 + v * (1.0 - s))
        h = hb[part, :]
        for j in range(0, chan, 256):
            cols = pl.ds(j, 256)
            v = dot(h, W2[:, :, :, cols].reshape(chan, 256), ((1,), (0,)))
            yb[part, cols] = (xr[part, cols].astype(F32) + v).astype(BF)

        @pl.when(seg < SECTIONS - 1)
        def _():
            y_next(m).start()

        @pl.when(y_direct(m))
        def _():
            y_skip(m).start()

        return carry

    lax.fori_loop(0, BLOCKS, forward, 0)

    @pl.when(seg == 3)
    def _():
        for m in range(early, BLOCKS):
            y_relay(m).start()

    @pl.when(seg == 0)
    def _():
        for m in range(BLOCKS):
            h_out(m).start()

    @pl.when(seg < 4)
    def _():
        transpose_weights()

    def turn():
        nT[...] = nb[...].T.reshape(nT.shape)
        hT[...] = hb[...].T.reshape(hT.shape)

    @pl.when(seg < 6)
    def _():
        turn()

    def backward(m, carry):
        part = pl.ds(pl.multiple_of(m * step, step), step)

        @pl.when(seg < SECTIONS - 1)
        def _():
            g_next(m).wait_recv()

        @pl.when(seg < 3)
        def _():
            g_skip(m).wait_recv()
            gr[part, :] = (gr[part, :].astype(F32) + gk[part, :].astype(F32)).astype(BF)

        @pl.when(seg == 0)
        def _():
            g_out(m).start()

        g = gr[part, :]
        for j in range(0, chan, 256):
            cols = pl.ds(j, 256)
            v = dot(g, T2[:, cols], ((1,), (0,)))
            dz[part, cols] = (v * sl[part, cols]).astype(BF)
        d = dz[part, :]
        for j in range(0, chan, 256):
            cols = pl.ds(j, 256)
            dn[:, cols] = dot(d, T1[:, cols], ((1,), (0,)))
        nrm = un[part, :]
        v = dn[...]
        along = jnp.mean(nrm * v, axis=-1, keepdims=True)
        r = rr[part, pl.ds(0, 1)]
        dx[part, :] = (g.astype(F32) + r * (v - nrm * along)).astype(BF)

        @pl.when(seg > 0)
        def _():
            g_next(m).start()

        @pl.when(g_direct(m))
        def _():
            g_skip(m).start()

        return carry

    lax.fori_loop(0, BLOCKS, backward, 0)

    @pl.when(seg == 4)
    def _():
        for m in range(early, BLOCKS):
            g_relay(m).start()

    dx_out = pltpu.make_async_copy(dx, dxo.at[0], lsem.at[6])
    dx_out.start()

    @pl.when(seg >= 6)
    def _():
        turn()

    sunits = [(w, h) for w in (1, 0, 2) for h in range(2)]
    FAR = (2, 1, -1, 0)

    def product(u, i):
        w, h = sunits[u]
        left, right, to = ((nT, dz, G1), (hT, gr, G2), (hU, gz, G3))[w]
        at = offs[axes[h][0]](FAR[i])
        at = (slice(None), at) if h == 0 else (at, slice(None))
        v = dot(left[at[0], at[1]].reshape(320, rows), right[:, pl.ds(*HALVES[h])], ((1,), (0,)))
        to[at[0], at[1], :, pl.ds(*HALVES[h])] = v.astype(BF).reshape(4, 80, 640)

    def block(u, first, second, part=ALL):
        w, h = sunits[u]
        return one((G1, G2, G3)[w], h, offs[axes[h][0]](first), offs[axes[h][1]](second), part)

    def scopy(u, kind, src, dst, leg, way):
        k = u * 16 + kind
        return pltpu.make_async_remote_copy(
            src_ref=src, dst_ref=dst, send_sem=ssend.at[k], recv_sem=srecv.at[k],
            device_id=dev(axes[sunits[u][1]][leg], way),
        )

    def out_way(i):
        return 1 if i < 2 else -1

    def opposite(u, i):
        return scopy(u, i, block(u, FAR[i], 2), r1.at[u, i], 1, out_way(i))

    def beside(u, i, way):
        k = 4 + 2 * i + (way < 0)
        return scopy(u, k, block(u, FAR[i], way), r2.at[u, i, int(way < 0)], 1, way)

    def last_opposite(u, way):
        part = TOP if way > 0 else LOW
        return scopy(u, 12 + (way < 0), block(u, 2, 0, part), r4.at[u, part], 0, way)

    def last_beside(u, way):
        return scopy(u, 14 + (way < 0), block(u, way, 0), r5.at[u, int(way < 0)], 0, way)

    def add(ref, *values):
        total = ref[...].astype(F32)
        for value in values:
            total = total + value.astype(F32)
        ref[...] = total.astype(BF)

    def leave(u, i):
        product(u, i)
        opposite(u, i).start()
        beside(u, i, -out_way(i)).start()

    def go_beside(u, i):
        way = out_way(i)
        opposite(u, i).wait_recv()
        add(block(u, FAR[i], way), r1[u, i])
        beside(u, i, way).start()

    def arrive(u, i):
        beside(u, i, 1).wait_recv()
        beside(u, i, -1).wait_recv()
        if i < 3:
            add(block(u, FAR[i], 0), r2[u, i, 0], r2[u, i, 1])
        if i == 0:
            last_opposite(u, 1).start()
            last_opposite(u, -1).start()
        elif i < 3:
            way = FAR[i]
            part = TOP if way > 0 else LOW
            last_opposite(u, way).wait_recv()
            add(block(u, way, 0, part), r4[u, part])
            last_beside(u, way).start()
        else:
            last_beside(u, 1).wait_recv()
            last_beside(u, -1).wait_recv()
            w, h = sunits[u]
            total = block(u, 0, 0)[...].astype(F32)
            for value in (r2[u, i, 0], r2[u, i, 1], r5[u, 0], r5[u, 1]):
                total = total + value.astype(F32)
            to = (acc1, acc2, accb)[w]
            to[:, pl.ds(*HALVES[h])] = total.astype(to.dtype)

    def ours(u, do):
        if u < 2:
            pl.when(seg != 0)(do)
        else:
            do()

    def group(units, *steps):
        for u in units:
            ours(u, lambda: [step(u, i) for step, i in steps] and None)

    def result(h):
        part = pl.ds(*HALVES[h])
        return pltpu.make_async_remote_copy(
            src_ref=accb.at[:, part], dst_ref=accr.at[:, part],
            send_sem=ssend.at[96 + h], recv_sem=srecv.at[96 + h],
            device_id={"segment": lax.rem(seg + SECTIONS - HELPER, SECTIONS)},
        )

    def helper(do):
        pl.when(seg == HELPER)(do)

    def take_over():
        for m in range(BLOCKS):
            h_out(m).wait_recv()
            g_out(m).wait_recv()
        hU[...] = hz[...].T.reshape(hU.shape)
        group(more, (leave, 0), (leave, 2))
        group(more, (leave, 1), (leave, 3))

    def give_back():
        group(more, (go_beside, 1), (go_beside, 3))
        for i in (2, 1, 3):
            group(more, (arrive, i))
        result(0).start()
        result(1).start()

    own, more = range(4), range(4, 6)
    group(own, (leave, 0), (leave, 2))
    group(own, (go_beside, 0), (go_beside, 2))
    group(own, (leave, 1), (leave, 3))
    group(own, (arrive, 0))
    group(own, (go_beside, 1), (go_beside, 3))
    group(own, (arrive, 2))
    helper(take_over)
    group(own, (arrive, 1))
    helper(lambda: group(more, (go_beside, 0), (go_beside, 2), (arrive, 0)))
    group(own, (arrive, 3))
    helper(give_back)

    @pl.when(seg == 0)
    def _():
        for h in range(2):
            result(h).wait_recv()
        acc2[...] = accr[...].astype(F32)

    out1 = pltpu.make_async_copy(acc1, fg.at[0], lsem.at[7])
    out2 = pltpu.make_async_copy(acc2, sg.at[0], lsem.at[8])
    out1.start()
    out2.start()

    def scattered(u):
        for k in range(4):
            opposite(u, k).wait_send()
            beside(u, k, 1).wait_send()
            beside(u, k, -1).wait_send()
        for way in (1, -1):
            last_opposite(u, way).wait_send()
            last_beside(u, way).wait_send()

    for u in range(4):
        for k in range(4):
            first_leg(u, k).wait_send()
            second_leg(u, k, 1).wait_send()
            second_leg(u, k, -1).wait_send()
            second_on(u, k).wait_send()
        ours(u, lambda: scattered(u))

    @pl.when(seg == HELPER)
    def _():
        for h in range(2):
            scattered(4 + h)
            result(h).wait_send()

    @pl.when(seg == 0)
    def _():
        for m in range(BLOCKS):
            h_out(m).wait_send()
            g_out(m).wait_send()

    @pl.when(seg == 3)
    def _():
        for m in range(early, BLOCKS):
            y_relay(m).wait_send()

    @pl.when(seg == 4)
    def _():
        for m in range(early, BLOCKS):
            g_relay(m).wait_send()

    def sent(m, carry):
        @pl.when(seg < SECTIONS - 1)
        def _():
            y_next(m).wait_send()

        @pl.when(y_direct(m))
        def _():
            y_skip(m).wait_send()

        @pl.when(seg > 0)
        def _():
            g_next(m).wait_send()

        @pl.when(g_direct(m))
        def _():
            g_skip(m).wait_send()

        return carry

    lax.fori_loop(0, BLOCKS, sent, 0)
    dx_out.wait()
    out1.wait()
    out2.wait()


def hand_over(a, b, c, out_a, out_b, out_c):
    out_a[...] = a[...]
    out_b[...] = b[...]
    out_c[...] = c[...]


def local(tokens, grad_out, first_weight, second_weight, emb_table, level_scale, timesteps, levels):
    rows, chan = tokens.shape
    depth = first_weight.shape[1]
    step = rows // BLOCKS
    samples = timesteps.shape[0]
    full = (RING, RING, depth, chan)
    vm = pltpu.VMEM
    dma = pltpu.SemaphoreType.DMA
    act = vm((rows, chan), BF)
    act32 = vm((rows, chan), F32)
    anyspec = pl.BlockSpec(memory_space=pl.ANY)
    vmspec = pl.BlockSpec(memory_space=pltpu.VMEM)
    smem = pl.BlockSpec(memory_space=pltpu.SMEM)
    macs = 6 * rows * chan * chan
    results = pl.pallas_call(
        kernel,
        out_shape=(
            jax.ShapeDtypeStruct((1, depth, chan), F32),
            jax.ShapeDtypeStruct((1, depth, chan), F32),
            jax.ShapeDtypeStruct((1, rows, chan), BF),
        ),
        in_specs=[anyspec] * 6 + [smem] * 2,
        out_specs=(anyspec,) * 3,
        scratch_shapes=[
            vm(full, BF), vm(full, BF), vm((chan, chan), BF), vm((chan, chan), BF),
            vm(full, BF), vm(full, BF),
            vm((RING, RING, depth, rows), BF), vm((RING, RING, depth, rows), BF),
            act, act, act, act, act, act32, act32, act, act, act,
            vm((step, chan), F32), act, vm((rows, 128), F32), vm((samples, chan), F32),
            act, act, vm((RING, RING, depth, rows), BF), vm(full, BF),
            vm((depth, chan), BF), vm((depth, chan), BF),
            vm(emb_table.shape, F32), vm(level_scale.shape, F32),
            vm((depth, chan), F32), vm((depth, chan), F32),
            vm((6, 4, depth, 640), BF), vm((6, 4, 2, depth, 640), BF),
            vm((6, depth, 640), BF), vm((6, 2, depth, 640), BF),
            dma((64,)), dma((64,)), dma((100,)), dma((100,)),
            dma((6 * BLOCKS,)), dma((6 * BLOCKS,)), dma((9,)), pltpu.SemaphoreType.REGULAR,
        ],
        compiler_params=pltpu.CompilerParams(
            collective_id=0, has_side_effects=True, vmem_limit_bytes=60 * 1024 * 1024
        ),
        cost_estimate=pl.CostEstimate(
            flops=2 * macs, bytes_accessed=16 * 1024 * 1024, transcendentals=rows * chan
        ),
        name="sections",
    )(tokens, grad_out, first_weight, second_weight, emb_table, level_scale, timesteps, levels)
    return pl.pallas_call(
        hand_over,
        out_shape=tuple(jax.ShapeDtypeStruct(r.shape, r.dtype) for r in results),
        in_specs=[vmspec] * 3,
        out_specs=(vmspec,) * 3,
        name="hand_over",
    )(*results)


def solution(mesh):
    weights = P("segment", "dp", None)
    in_specs = (P("dp", None), P("dp", None), weights, weights, P(), P(), P("dp"), P("segment"))
    out_specs = (weights, weights, weights)
    return jax.shard_map(local, mesh=mesh, in_specs=in_specs, out_specs=out_specs, check_vma=False)
```

```python
import functools

import jax
import jax.numpy as jnp
from jax import lax
from jax.experimental import pallas as pl
from jax.experimental.pallas import tpu as pltpu
from jax.sharding import PartitionSpec as P

EPS = 1e-06
SECTIONS = 8
RING = 4
HELPER = 7
BLOCKS = 4
TILE = 128
HALVES = ((0, 640), (640, 640))
F32 = jnp.float32
BF = jnp.bfloat16


def dot(a, b, contract):
    return lax.dot_general(a, b, (contract, ((), ())), preferred_element_type=F32)


def kernel(
    tok, go, w1, w2, emb, lvl, ts, lv,
    fg, sg, dxo,
    W1, W2, T1, T2, G1, G2, nT, hT,
    xr, sk, yb, nb, hb, un, sl, gr, gk, dz, dn, dx, rr, cond,
    hz, gz, hU, G3, accb, accr, part2,
    embv, lvlv, r1, r2, r4, r5,
    gsend, grecv, ssend, srecv, psend, precv, lsem, turn_sem,
):
    seg = lax.axis_index("segment")
    dp = lax.axis_index("dp")
    z, x = dp // RING, dp % RING
    rows, chan = xr.shape
    step = rows // BLOCKS
    samples = ts.shape[0]

    def at_z(i):
        return lax.rem(z + i + RING, RING)

    def at_x(i):
        return lax.rem(x + i + RING, RING)

    def dev(axis, i):
        return {"dp": at_z(i) * RING + x} if axis == "z" else {"dp": z * RING + at_x(i)}

    own1 = pltpu.make_async_copy(w1.at[0], W1.at[z, x], lsem.at[0])
    own2 = pltpu.make_async_copy(w2.at[0], W2.at[z, x], lsem.at[1])
    table = pltpu.make_async_copy(emb, embv, lsem.at[2])
    scales = pltpu.make_async_copy(lvl, lvlv, lsem.at[3])
    own1.start()
    own2.start()
    table.start()
    scales.start()
    tok_in = pltpu.make_async_copy(tok, xr, lsem.at[4])
    go_in = pltpu.make_async_copy(go, gr, lsem.at[5])

    @pl.when(seg == 0)
    def _():
        tok_in.start()

    @pl.when(seg == SECTIONS - 1)
    def _():
        go_in.start()

    barrier = pltpu.get_barrier_semaphore()
    for axis in ("z", "x"):
        for way in (1, -1):
            pl.semaphore_signal(barrier, inc=1, device_id=dev(axis, way))

    @pl.when(seg > 0)
    def _():
        pl.semaphore_signal(barrier, inc=1, device_id={"segment": seg - 1})

    @pl.when(seg < SECTIONS - 1)
    def _():
        pl.semaphore_signal(barrier, inc=1, device_id={"segment": seg + 1})

    relay = jnp.logical_and(seg > 1, seg < 6)

    @pl.when(relay)
    def _():
        pl.semaphore_signal(barrier, inc=1, device_id={"segment": jnp.where(seg < 4, seg + 2, seg - 2)})

    helped = jnp.logical_or(seg == 1, seg == HELPER)

    @pl.when(helped)
    def _():
        pl.semaphore_signal(barrier, inc=1, device_id={"segment": 1 + HELPER - seg})

    far = jnp.logical_or(seg < 3, seg > 4)

    @pl.when(far)
    def _():
        pl.semaphore_signal(barrier, inc=1, device_id={"segment": SECTIONS - 1 - seg})

    pl.semaphore_wait(
        barrier,
        4
        + (seg > 0).astype(jnp.int32)
        + (seg < SECTIONS - 1).astype(jnp.int32)
        + far.astype(jnp.int32)
        + relay.astype(jnp.int32)
        + helped.astype(jnp.int32),
    )
    own1.wait()
    own2.wait()

    units = [(w, h) for w in range(2) for h in range(2)] + [(2, 1)]
    axes = (("x", "z"), ("z", "x"))
    offs = {"x": at_x, "z": at_z}
    ALL, TOP, LOW = pl.ds(0, 80), pl.ds(0, 48), pl.ds(48, 32)

    def one(ref, h, first, second, part=ALL):
        i = (second, first) if h == 0 else (first, second)
        return ref.at[i[0], i[1], part, pl.ds(*HALVES[h])]

    def gcopy(u, kind, first, second, part, leg, way):
        w, h = units[u]
        at = (offs[axes[h][0]](first), offs[axes[h][1]](second))
        if w == 2:
            ref = part2.at[at[0], at[1], part]
        else:
            ref = one((W1, W2)[w], h, *at, part)
        k = u * 16 + kind
        return pltpu.make_async_remote_copy(
            src_ref=ref, dst_ref=ref, send_sem=gsend.at[k], recv_sem=grecv.at[k],
            device_id=dev(axes[h][leg], way),
        )

    NEAR = (0, -1, 1, 2)

    def first_leg(u, kind):
        return gcopy(
            u, kind, (0, 0, -1, 1)[kind], 0, (ALL, ALL, TOP, LOW)[kind], 0, (1, -1, 1, -1)[kind]
        )

    def second_leg(u, i, way):
        return gcopy(u, 4 + 2 * i + (way < 0), NEAR[i], 0, ALL, 1, way)

    def second_on(u, i):
        way = 1 if i < 2 else -1
        return gcopy(u, 12 + i, NEAR[i], -way, ALL, 1, way)

    def spread(u, i):
        second_leg(u, i, 1).start()
        second_leg(u, i, -1).start()

    def pass_on(u, i):
        second_leg(u, i, 1 if i < 2 else -1).wait_recv()
        second_on(u, i).start()

    PLACES = (0, -1, 1, 2)

    def hand(i, j):
        at = (at_z(NEAR[i]), at_x(PLACES[j]))
        there = W2.at[at[0], at[1], :, pl.ds(*HALVES[1])]
        src, dst, to = (part2.at[at[0], at[1]], there, 1) if i + j else (there, part2.at[z, x], HELPER)
        k = 80 + 4 * i + j
        return pltpu.make_async_remote_copy(
            src_ref=src, dst_ref=dst, send_sem=gsend.at[k], recv_sem=grecv.at[k],
            device_id={"segment": to},
        )

    def gather_for_another():
        hand(0, 0).wait_recv()
        first_leg(4, 0).start()
        first_leg(4, 1).start()
        spread(4, 0)
        first_leg(4, 0).wait_recv()
        first_leg(4, 2).start()
        first_leg(4, 1).wait_recv()
        first_leg(4, 3).start()
        spread(4, 1)
        spread(4, 2)
        hand(1, 0).start()
        hand(2, 0).start()
        pass_on(4, 0)
        hand(0, 1).start()
        first_leg(4, 2).wait_recv()
        first_leg(4, 3).wait_recv()
        spread(4, 3)
        hand(3, 0).start()
        for i in range(1, 4):
            pass_on(4, i)
            hand(i, 1 if i < 2 else 2).start()
        for i in range(4):
            second_leg(4, i, -1 if i < 2 else 1).wait_recv()
            hand(i, 2 if i < 2 else 1).start()
            second_on(4, i).wait_recv()
            hand(i, 3).start()

    @pl.when(seg == 1)
    def _():
        hand(0, 0).start()

    @pl.when(seg == HELPER)
    def _():
        gather_for_another()

    odd = lax.rem(seg, 2) == 1

    @pl.when(odd)
    def _():
        pl.semaphore_wait(turn_sem, 1)

    def each(do):
        for u in range(4):
            if u == 3:
                pl.when(seg != 1)(lambda: do(3))
            else:
                do(u)

    def begin(u):
        first_leg(u, 0).start()
        first_leg(u, 1).start()

    def onward(u):
        first_leg(u, 0).wait_recv()
        first_leg(u, 2).start()
        first_leg(u, 1).wait_recv()
        first_leg(u, 3).start()
        spread(u, 1)
        spread(u, 2)

    def across(u):
        pass_on(u, 0)
        first_leg(u, 2).wait_recv()
        first_leg(u, 3).wait_recv()
        spread(u, 3)

    def whole(u):
        for i in range(4):
            second_leg(u, i, -1 if i < 2 else 1).wait_recv()
            second_on(u, i).wait_recv()

    each(begin)
    each(lambda u: spread(u, 0))
    each(onward)
    each(across)

    @pl.when(jnp.logical_not(odd))
    def _():
        pl.semaphore_signal(turn_sem, inc=1, device_id={"segment": lax.rem(seg + 1, SECTIONS)})

    for i in range(1, 4):
        each(lambda u: pass_on(u, i))

    table.wait()
    scales.wait()
    scale_row = lvlv[pl.ds(lv[0], 1), :]
    for i in range(samples):
        cond[pl.ds(i, 1), :] = embv[pl.ds(ts[i], 1), :] * scale_row

    @pl.when(seg == 0)
    def _():
        tok_in.wait()

    @pl.when(seg == SECTIONS - 1)
    def _():
        go_in.wait()

    each(whole)

    @pl.when(seg == 1)
    def _():
        for k in range(1, 16):
            hand(k // 4, k % 4).wait_recv()

    def transpose_weights():
        for j in range(0, chan, 256):
            T1[pl.ds(j, 256), :] = W1[:, :, :, pl.ds(j, 256)].reshape(chan, 256).T
            T2[pl.ds(j, 256), :] = W2[:, :, :, pl.ds(j, 256)].reshape(chan, 256).T

    @pl.when(seg >= 4)
    def _():
        transpose_weights()

    def pcopy(kind, m, src, dst, to, cols=(0, 1280)):
        k = kind * BLOCKS + m
        part = pl.ds(pl.multiple_of(m * step, step), step)
        return pltpu.make_async_remote_copy(
            src_ref=src.at[part, pl.ds(*cols)], dst_ref=dst.at[part, pl.ds(*cols)],
            send_sem=psend.at[k], recv_sem=precv.at[k], device_id={"segment": to},
        )

    def y_next(m, i):
        return pcopy((0, 6)[i], m, yb, xr, lax.rem(seg + 1, SECTIONS), HALVES[i])

    def y_skip(m):
        return pcopy(1, m, yb, sk, SECTIONS - 1 - seg)

    def g_next(m):
        return pcopy(2, m, dx, gr, lax.rem(seg + SECTIONS - 1, SECTIONS))

    def g_skip(m):
        return pcopy(3, m, dx, gk, SECTIONS - 1 - seg)

    def y_relay(m):
        return pcopy(1, m, xr, sk, lax.rem(seg + 2, SECTIONS))

    def g_relay(m):
        return pcopy(3, m, gr, gk, lax.rem(seg + SECTIONS - 2, SECTIONS))

    def h_out(m):
        return pcopy(4, m, hb, hz, HELPER)

    def g_out(m):
        return pcopy(5, m, gr, gz, HELPER)

    early = BLOCKS // 2

    def y_direct(m):
        return jnp.logical_or(seg < 2, jnp.logical_and(seg == 2, m < early))

    def g_direct(m):
        return jnp.logical_or(seg > 5, jnp.logical_and(seg == 5, m < early))

    def forward(m, carry):
        part = pl.ds(pl.multiple_of(m * step, step), step)

        @pl.when(seg > 0)
        def _():
            y_next(m, 0).wait_recv()
            y_next(m, 1).wait_recv()

        @pl.when(seg > 4)
        def _():
            y_skip(m).wait_recv()
            xr[part, :] = (xr[part, :].astype(F32) + sk[part, :].astype(F32)).astype(BF)

        row = cond[pl.ds(m // (BLOCKS // samples), 1), :]
        u = xr[part, :].astype(F32) + row
        r = lax.rsqrt(jnp.mean(u * u, axis=-1, keepdims=True) + EPS)
        un[part, :] = u * r
        rr[part, :] = jnp.broadcast_to(r, (step, 128))
        n = (u * r).astype(BF)
        nb[part, :] = n
        for j in range(0, chan, TILE):
            cols = pl.ds(j, TILE)
            v = dot(n, W1[:, :, :, cols].reshape(chan, TILE), ((1,), (0,)))
            s = jax.nn.sigmoid(v)
            hb[part, cols] = (v * s).astype(BF)
            sl[part, cols] = s * (1.0 + v * (1.0 - s))
        h = hb[part, :]
        for i, half in enumerate(HALVES):
            cols = pl.ds(*half)
            v = dot(h, W2[:, :, :, cols].reshape(chan, 640), ((1,), (0,)))
            yb[part, cols] = (xr[part, cols].astype(F32) + v).astype(BF)

            @pl.when(seg < SECTIONS - 1)
            def _():
                y_next(m, i).start()

        @pl.when(y_direct(m))
        def _():
            y_skip(m).start()

        return carry

    lax.fori_loop(0, BLOCKS, forward, 0)

    @pl.when(seg == 3)
    def _():
        for m in range(early, BLOCKS):
            y_relay(m).start()

    @pl.when(seg == 0)
    def _():
        for m in range(BLOCKS):
            h_out(m).start()

    @pl.when(seg < 4)
    def _():
        transpose_weights()

    def turn():
        nT[...] = nb[...].T.reshape(nT.shape)
        hT[...] = hb[...].T.reshape(hT.shape)

    @pl.when(seg < 6)
    def _():
        turn()

    def backward(m, carry):
        part = pl.ds(pl.multiple_of(m * step, step), step)

        @pl.when(seg < SECTIONS - 1)
        def _():
            g_next(m).wait_recv()

        @pl.when(seg < 3)
        def _():
            g_skip(m).wait_recv()
            gr[part, :] = (gr[part, :].astype(F32) + gk[part, :].astype(F32)).astype(BF)

        @pl.when(seg == 0)
        def _():
            g_out(m).start()

        g = gr[part, :]
        for j in range(0, chan, TILE):
            cols = pl.ds(j, TILE)
            v = dot(g, T2[:, cols], ((1,), (0,)))
            dz[part, cols] = (v * sl[part, cols]).astype(BF)
        d = dz[part, :]
        for half in HALVES:
            cols = pl.ds(*half)
            dn[:, cols] = dot(d, T1[:, cols], ((1,), (0,)))
        nrm = un[part, :]
        v = dn[...]
        along = jnp.mean(nrm * v, axis=-1, keepdims=True)
        r = rr[part, pl.ds(0, 1)]
        dx[part, :] = (g.astype(F32) + r * (v - nrm * along)).astype(BF)

        @pl.when(seg > 0)
        def _():
            g_next(m).start()

        @pl.when(g_direct(m))
        def _():
            g_skip(m).start()

        return carry

    lax.fori_loop(0, BLOCKS, backward, 0)

    @pl.when(seg == 4)
    def _():
        for m in range(early, BLOCKS):
            g_relay(m).start()

    dx_out = pltpu.make_async_copy(dx, dxo.at[0], lsem.at[6])
    dx_out.start()

    @pl.when(seg >= 6)
    def _():
        turn()

    sunits = [(w, h) for w in (1, 0, 2) for h in range(2)]
    FAR = (2, 1, -1, 0)

    def product(u, i):
        w, h = sunits[u]
        left, right, to = ((nT, dz, G1), (hT, gr, G2), (hU, gz, G3))[w]
        at = offs[axes[h][0]](FAR[i])
        at = (slice(None), at) if h == 0 else (at, slice(None))
        v = dot(left[at[0], at[1]].reshape(320, rows), right[:, pl.ds(*HALVES[h])], ((1,), (0,)))
        to[at[0], at[1], :, pl.ds(*HALVES[h])] = v.astype(BF).reshape(4, 80, 640)

    def block(u, first, second, part=ALL):
        w, h = sunits[u]
        return one((G1, G2, G3)[w], h, offs[axes[h][0]](first), offs[axes[h][1]](second), part)

    def scopy(u, kind, src, dst, leg, way):
        k = u * 16 + kind
        return pltpu.make_async_remote_copy(
            src_ref=src, dst_ref=dst, send_sem=ssend.at[k], recv_sem=srecv.at[k],
            device_id=dev(axes[sunits[u][1]][leg], way),
        )

    def out_way(i):
        return 1 if i < 2 else -1

    def opposite(u, i):
        return scopy(u, i, block(u, FAR[i], 2), r1.at[u, i], 1, out_way(i))

    def beside(u, i, way):
        k = 4 + 2 * i + (way < 0)
        return scopy(u, k, block(u, FAR[i], way), r2.at[u, i, int(way < 0)], 1, way)

    def last_opposite(u, way):
        part = TOP if way > 0 else LOW
        return scopy(u, 12 + (way < 0), block(u, 2, 0, part), r4.at[u, part], 0, way)

    def last_beside(u, way):
        return scopy(u, 14 + (way < 0), block(u, way, 0), r5.at[u, int(way < 0)], 0, way)

    def add(ref, *values):
        total = ref[...].astype(F32)
        for value in values:
            total = total + value.astype(F32)
        ref[...] = total.astype(BF)

    def leave(u, i):
        product(u, i)
        opposite(u, i).start()
        beside(u, i, -out_way(i)).start()

    def go_beside(u, i):
        way = out_way(i)
        opposite(u, i).wait_recv()
        add(block(u, FAR[i], way), r1[u, i])
        beside(u, i, way).start()

    def arrive(u, i):
        beside(u, i, 1).wait_recv()
        beside(u, i, -1).wait_recv()
        if i < 3:
            add(block(u, FAR[i], 0), r2[u, i, 0], r2[u, i, 1])
        if i == 0:
            last_opposite(u, 1).start()
            last_opposite(u, -1).start()
        elif i < 3:
            way = FAR[i]
            part = TOP if way > 0 else LOW
            last_opposite(u, way).wait_recv()
            add(block(u, way, 0, part), r4[u, part])
            last_beside(u, way).start()
        else:
            last_beside(u, 1).wait_recv()
            last_beside(u, -1).wait_recv()
            w, h = sunits[u]
            total = block(u, 0, 0)[...].astype(F32)
            for value in (r2[u, i, 0], r2[u, i, 1], r5[u, 0], r5[u, 1]):
                total = total + value.astype(F32)
            to = (fg.at[0], sg.at[0], accb)[w]
            to[:, pl.ds(*HALVES[h])] = total.astype(to.dtype)

    def ours(u, do):
        if u < 2:
            pl.when(seg != 0)(do)
        else:
            do()

    def group(units, *steps):
        for u in units:
            ours(u, lambda: [step(u, i) for step, i in steps] and None)

    def result(h):
        part = pl.ds(*HALVES[h])
        return pltpu.make_async_remote_copy(
            src_ref=accb.at[:, part], dst_ref=accr.at[:, part],
            send_sem=ssend.at[96 + h], recv_sem=srecv.at[96 + h],
            device_id={"segment": lax.rem(seg + SECTIONS - HELPER, SECTIONS)},
        )

    def helper(do):
        pl.when(seg == HELPER)(do)

    def take_over():
        for m in range(BLOCKS):
            h_out(m).wait_recv()
            g_out(m).wait_recv()
        hU[...] = hz[...].T.reshape(hU.shape)
        group(more, (leave, 0), (leave, 2))
        group(more, (leave, 1), (leave, 3))

    def give_back():
        group(more, (go_beside, 1), (go_beside, 3))
        for i in (2, 1, 3):
            group(more, (arrive, i))
        result(0).start()
        result(1).start()

    own, more = range(4), range(4, 6)
    group(own, (leave, 0))
    group(own, (leave, 2))
    group(own, (go_beside, 0))
    group(own, (leave, 1))
    group(own, (go_beside, 2))
    group(own, (arrive, 0))
    group(own, (leave, 3))
    group(own, (go_beside, 1))
    group(own, (arrive, 2))
    group(own, (go_beside, 3))
    group(own, (arrive, 1))
    helper(take_over)
    helper(lambda: group(more, (go_beside, 0), (go_beside, 2), (arrive, 0)))
    helper(give_back)
    group(own, (arrive, 3))

    @pl.when(seg == 0)
    def _():
        for h in range(2):
            result(h).wait_recv()
        sg[0] = accr[...].astype(F32)

    def scattered(u):
        for k in range(4):
            opposite(u, k).wait_send()
            beside(u, k, 1).wait_send()
            beside(u, k, -1).wait_send()
        for way in (1, -1):
            last_opposite(u, way).wait_send()
            last_beside(u, way).wait_send()

    def gathered(u):
        for k in range(4):
            first_leg(u, k).wait_send()
            second_leg(u, k, 1).wait_send()
            second_leg(u, k, -1).wait_send()
            second_on(u, k).wait_send()

    each(gathered)
    for u in range(4):
        ours(u, lambda: scattered(u))

    @pl.when(seg == 1)
    def _():
        hand(0, 0).wait_send()

    @pl.when(seg == HELPER)
    def _():
        gathered(4)
        for k in range(1, 16):
            hand(k // 4, k % 4).wait_send()

    @pl.when(seg == HELPER)
    def _():
        for h in range(2):
            scattered(4 + h)
            result(h).wait_send()

    @pl.when(seg == 0)
    def _():
        for m in range(BLOCKS):
            h_out(m).wait_send()
            g_out(m).wait_send()

    @pl.when(seg == 3)
    def _():
        for m in range(early, BLOCKS):
            y_relay(m).wait_send()

    @pl.when(seg == 4)
    def _():
        for m in range(early, BLOCKS):
            g_relay(m).wait_send()

    def sent(m, carry):
        @pl.when(seg < SECTIONS - 1)
        def _():
            y_next(m, 0).wait_send()
            y_next(m, 1).wait_send()

        @pl.when(y_direct(m))
        def _():
            y_skip(m).wait_send()

        @pl.when(seg > 0)
        def _():
            g_next(m).wait_send()

        @pl.when(g_direct(m))
        def _():
            g_skip(m).wait_send()

        return carry

    lax.fori_loop(0, BLOCKS, sent, 0)
    dx_out.wait()


def local(tokens, grad_out, first_weight, second_weight, emb_table, level_scale, timesteps, levels):
    rows, chan = tokens.shape
    depth = first_weight.shape[1]
    step = rows // BLOCKS
    samples = timesteps.shape[0]
    full = (RING, RING, depth, chan)
    vm = pltpu.VMEM
    dma = pltpu.SemaphoreType.DMA
    act = vm((rows, chan), BF)
    act32 = vm((rows, chan), F32)
    anyspec = pl.BlockSpec(memory_space=pl.ANY)
    vmspec = pl.BlockSpec(memory_space=pltpu.VMEM)
    smem = pl.BlockSpec(memory_space=pltpu.SMEM)
    macs = 6 * rows * chan * chan
    return pl.pallas_call(
        kernel,
        out_shape=(
            vm((1, depth, chan), F32),
            vm((1, depth, chan), F32),
            vm((1, rows, chan), BF),
        ),
        in_specs=[anyspec] * 6 + [smem] * 2,
        out_specs=(vmspec,) * 3,
        scratch_shapes=[
            vm(full, BF), vm(full, BF), vm((chan, chan), BF), vm((chan, chan), BF),
            vm(full, BF), vm(full, BF),
            vm((RING, RING, depth, rows), BF), vm((RING, RING, depth, rows), BF),
            act, act, act, act, act, act32, act32, act, act, act,
            vm((step, chan), F32), act, vm((rows, 128), F32), vm((samples, chan), F32),
            act, act, vm((RING, RING, depth, rows), BF), vm(full, BF),
            vm((depth, chan), BF), vm((depth, chan), BF), vm((RING, RING, depth, 640), BF),
            vm(emb_table.shape, F32), vm(level_scale.shape, F32),
            vm((6, 4, depth, 640), BF), vm((6, 4, 2, depth, 640), BF),
            vm((6, depth, 640), BF), vm((6, 2, depth, 640), BF),
            dma((96,)), dma((96,)), dma((100,)), dma((100,)),
            dma((7 * BLOCKS,)), dma((7 * BLOCKS,)), dma((7,)), pltpu.SemaphoreType.REGULAR,
        ],
        compiler_params=pltpu.CompilerParams(
            collective_id=0, has_side_effects=True, vmem_limit_bytes=60 * 1024 * 1024
        ),
        cost_estimate=pl.CostEstimate(
            flops=2 * macs, bytes_accessed=16 * 1024 * 1024, transcendentals=rows * chan
        ),
        name="sections",
    )(tokens, grad_out, first_weight, second_weight, emb_table, level_scale, timesteps, levels)


def solution(mesh):
    weights = P("segment", "dp", None)
    in_specs = (P("dp", None), P("dp", None), weights, weights, P(), P(), P("dp"), P("segment"))
    out_specs = (weights, weights, weights)
    return jax.shard_map(local, mesh=mesh, in_specs=in_specs, out_specs=out_specs, check_vma=False)
```

```python
import functools

import jax
import jax.numpy as jnp
from jax import lax
from jax.experimental import pallas as pl
from jax.experimental.pallas import tpu as pltpu
from jax.sharding import PartitionSpec as P

EPS = 1e-06
SECTIONS = 8
RING = 4
HELPER = 7
BLOCKS = 4
TILE = 128
HALVES = ((0, 640), (640, 640))
F32 = jnp.float32
BF = jnp.bfloat16


def dot(a, b, contract):
    return lax.dot_general(a, b, (contract, ((), ())), preferred_element_type=F32)


def kernel(
    tok, go, w1, w2, emb, lvl, ts, lv,
    fg, sg, dxo,
    W1, W2, T1, T2, G1, G2, nT, hT,
    xr, sk, yb, nb, hb, un, sl, gr, gk, dz, dn, dx, rr, cond,
    hz, gz, hU, G3, accb, accr, part2,
    embv, lvlv, r1, r2, r4, r5,
    gsend, grecv, ssend, srecv, psend, precv, lsem, turn_sem,
):
    seg = lax.axis_index("segment")
    dp = lax.axis_index("dp")
    z, x = dp // RING, dp % RING
    rows, chan = xr.shape
    step = rows // BLOCKS
    samples = ts.shape[0]

    def at_z(i):
        return lax.rem(z + i + RING, RING)

    def at_x(i):
        return lax.rem(x + i + RING, RING)

    def dev(axis, i):
        return {"dp": at_z(i) * RING + x} if axis == "z" else {"dp": z * RING + at_x(i)}

    own1 = pltpu.make_async_copy(w1.at[0], W1.at[z, x], lsem.at[0])
    own2 = pltpu.make_async_copy(w2.at[0], W2.at[z, x], lsem.at[1])
    table = pltpu.make_async_copy(emb, embv, lsem.at[2])
    scales = pltpu.make_async_copy(lvl, lvlv, lsem.at[3])
    own1.start()
    own2.start()
    table.start()
    scales.start()
    tok_in = pltpu.make_async_copy(tok, xr, lsem.at[4])
    go_in = pltpu.make_async_copy(go, gr, lsem.at[5])

    @pl.when(seg == 0)
    def _():
        tok_in.start()

    @pl.when(seg == SECTIONS - 1)
    def _():
        go_in.start()

    barrier = pltpu.get_barrier_semaphore()
    for axis in ("z", "x"):
        for way in (1, -1):
            pl.semaphore_signal(barrier, inc=1, device_id=dev(axis, way))

    @pl.when(seg > 0)
    def _():
        pl.semaphore_signal(barrier, inc=1, device_id={"segment": seg - 1})

    @pl.when(seg < SECTIONS - 1)
    def _():
        pl.semaphore_signal(barrier, inc=1, device_id={"segment": seg + 1})

    relay = jnp.logical_and(seg > 1, seg < 6)

    @pl.when(relay)
    def _():
        pl.semaphore_signal(barrier, inc=1, device_id={"segment": jnp.where(seg < 4, seg + 2, seg - 2)})

    helped = jnp.logical_or(seg == 1, seg == HELPER)

    @pl.when(helped)
    def _():
        pl.semaphore_signal(barrier, inc=1, device_id={"segment": 1 + HELPER - seg})

    far = jnp.logical_or(seg < 3, seg > 4)

    @pl.when(far)
    def _():
        pl.semaphore_signal(barrier, inc=1, device_id={"segment": SECTIONS - 1 - seg})

    pl.semaphore_wait(
        barrier,
        4
        + (seg > 0).astype(jnp.int32)
        + (seg < SECTIONS - 1).astype(jnp.int32)
        + far.astype(jnp.int32)
        + relay.astype(jnp.int32)
        + helped.astype(jnp.int32),
    )
    own1.wait()
    own2.wait()

    units = [(w, h) for w in range(2) for h in range(2)] + [(2, 1)]
    axes = (("x", "z"), ("z", "x"))
    offs = {"x": at_x, "z": at_z}
    ALL, TOP, LOW = pl.ds(0, 80), pl.ds(0, 48), pl.ds(48, 32)

    def one(ref, h, first, second, part=ALL):
        i = (second, first) if h == 0 else (first, second)
        return ref.at[i[0], i[1], part, pl.ds(*HALVES[h])]

    def gcopy(u, kind, first, second, part, leg, way):
        w, h = units[u]
        at = (offs[axes[h][0]](first), offs[axes[h][1]](second))
        if w == 2:
            ref = part2.at[at[0], at[1], part]
        else:
            ref = one((W1, W2)[w], h, *at, part)
        k = u * 16 + kind
        return pltpu.make_async_remote_copy(
            src_ref=ref, dst_ref=ref, send_sem=gsend.at[k], recv_sem=grecv.at[k],
            device_id=dev(axes[h][leg], way),
        )

    NEAR = (0, -1, 1, 2)

    def share(u, way):
        return TOP if (way > 0) == (u % 4 < 2) else LOW

    def first_leg(u, kind):
        return gcopy(
            u, kind, (0, 0, -1, 1)[kind], 0, (ALL, ALL, share(u, 1), share(u, -1))[kind], 0, (1, -1, 1, -1)[kind]
        )

    def second_leg(u, i, way):
        return gcopy(u, 4 + 2 * i + (way < 0), NEAR[i], 0, ALL, 1, way)

    def second_on(u, i):
        way = 1 if i < 2 else -1
        return gcopy(u, 12 + i, NEAR[i], -way, ALL, 1, way)

    def spread(u, i):
        second_leg(u, i, 1).start()
        second_leg(u, i, -1).start()

    def pass_on(u, i):
        second_leg(u, i, 1 if i < 2 else -1).wait_recv()
        second_on(u, i).start()

    PLACES = (0, -1, 1, 2)

    def hand(i, j):
        at = (at_z(NEAR[i]), at_x(PLACES[j]))
        there = W2.at[at[0], at[1], :, pl.ds(*HALVES[1])]
        src, dst, to = (part2.at[at[0], at[1]], there, 1) if i + j else (there, part2.at[z, x], HELPER)
        k = 80 + 4 * i + j
        return pltpu.make_async_remote_copy(
            src_ref=src, dst_ref=dst, send_sem=gsend.at[k], recv_sem=grecv.at[k],
            device_id={"segment": to},
        )

    def gather_for_another():
        hand(0, 0).wait_recv()
        first_leg(4, 0).start()
        first_leg(4, 1).start()
        spread(4, 0)
        first_leg(4, 0).wait_recv()
        first_leg(4, 2).start()
        first_leg(4, 1).wait_recv()
        first_leg(4, 3).start()
        spread(4, 1)
        spread(4, 2)
        hand(1, 0).start()
        hand(2, 0).start()
        pass_on(4, 0)
        hand(0, 1).start()
        first_leg(4, 2).wait_recv()
        first_leg(4, 3).wait_recv()
        spread(4, 3)
        hand(3, 0).start()
        for i in range(1, 4):
            pass_on(4, i)
            hand(i, 1 if i < 2 else 2).start()
        for i in range(4):
            second_leg(4, i, -1 if i < 2 else 1).wait_recv()
            hand(i, 2 if i < 2 else 1).start()
            second_on(4, i).wait_recv()
            hand(i, 3).start()

    @pl.when(seg == 1)
    def _():
        hand(0, 0).start()

    @pl.when(seg == HELPER)
    def _():
        gather_for_another()

    odd = lax.rem(seg, 2) == 1

    @pl.when(odd)
    def _():
        pl.semaphore_wait(turn_sem, 1)

    def each(do):
        for u in range(4):
            if u == 3:
                pl.when(seg != 1)(lambda: do(3))
            else:
                do(u)

    def begin(u):
        first_leg(u, 0).start()
        first_leg(u, 1).start()

    def onward(u):
        first_leg(u, 0).wait_recv()
        first_leg(u, 2).start()
        first_leg(u, 1).wait_recv()
        first_leg(u, 3).start()
        spread(u, 1)
        spread(u, 2)

    def across(u):
        pass_on(u, 0)
        first_leg(u, 2).wait_recv()
        first_leg(u, 3).wait_recv()
        spread(u, 3)

    def whole(u):
        for i in range(4):
            second_leg(u, i, -1 if i < 2 else 1).wait_recv()
            second_on(u, i).wait_recv()

    each(begin)
    each(lambda u: spread(u, 0))
    each(onward)
    @pl.when(jnp.logical_not(odd))
    def _():
        pl.semaphore_signal(turn_sem, inc=1, device_id={"segment": lax.rem(seg + 1, SECTIONS)})

    each(across)

    for i in range(1, 4):
        each(lambda u: pass_on(u, i))

    table.wait()
    scales.wait()
    scale_row = lvlv[pl.ds(lv[0], 1), :]
    for i in range(samples):
        cond[pl.ds(i, 1), :] = embv[pl.ds(ts[i], 1), :] * scale_row

    @pl.when(seg == 0)
    def _():
        tok_in.wait()

    @pl.when(seg == SECTIONS - 1)
    def _():
        go_in.wait()

    each(whole)

    @pl.when(seg == 1)
    def _():
        for k in range(1, 16):
            hand(k // 4, k % 4).wait_recv()

    def transpose_weights():
        for j in range(0, chan, 256):
            T1[pl.ds(j, 256), :] = W1[:, :, :, pl.ds(j, 256)].reshape(chan, 256).T
            T2[pl.ds(j, 256), :] = W2[:, :, :, pl.ds(j, 256)].reshape(chan, 256).T

    @pl.when(seg >= 4)
    def _():
        transpose_weights()

    def pcopy(kind, m, src, dst, to, cols=(0, 1280)):
        k = kind * BLOCKS + m
        part = pl.ds(pl.multiple_of(m * step, step), step)
        return pltpu.make_async_remote_copy(
            src_ref=src.at[part, pl.ds(*cols)], dst_ref=dst.at[part, pl.ds(*cols)],
            send_sem=psend.at[k], recv_sem=precv.at[k], device_id={"segment": to},
        )

    def y_next(m, i):
        return pcopy((0, 6)[i], m, yb, xr, lax.rem(seg + 1, SECTIONS), HALVES[i])

    def y_skip(m):
        return pcopy(1, m, yb, sk, SECTIONS - 1 - seg)

    def g_next(m):
        return pcopy(2, m, dx, gr, lax.rem(seg + SECTIONS - 1, SECTIONS))

    def g_skip(m):
        return pcopy(3, m, dx, gk, SECTIONS - 1 - seg)

    def y_relay(m):
        return pcopy(1, m, xr, sk, lax.rem(seg + 2, SECTIONS))

    def g_relay(m):
        return pcopy(3, m, gr, gk, lax.rem(seg + SECTIONS - 2, SECTIONS))

    def h_out(m):
        return pcopy(4, m, hb, hz, HELPER)

    def g_out(m):
        return pcopy(5, m, gr, gz, HELPER)

    early = BLOCKS // 2

    def y_direct(m):
        return jnp.logical_or(seg < 2, jnp.logical_and(seg == 2, m < early))

    def g_direct(m):
        return jnp.logical_or(seg > 5, jnp.logical_and(seg == 5, m < early))

    def forward(m, carry):
        part = pl.ds(pl.multiple_of(m * step, step), step)

        @pl.when(seg > 0)
        def _():
            y_next(m, 0).wait_recv()
            y_next(m, 1).wait_recv()

        @pl.when(seg > 4)
        def _():
            y_skip(m).wait_recv()
            xr[part, :] = (xr[part, :].astype(F32) + sk[part, :].astype(F32)).astype(BF)

        row = cond[pl.ds(m // (BLOCKS // samples), 1), :]
        u = xr[part, :].astype(F32) + row
        r = lax.rsqrt(jnp.mean(u * u, axis=-1, keepdims=True) + EPS)
        un[part, :] = u * r
        rr[part, :] = jnp.broadcast_to(r, (step, 128))
        n = (u * r).astype(BF)
        nb[part, :] = n
        for j in range(0, chan, TILE):
            cols = pl.ds(j, TILE)
            v = dot(n, W1[:, :, :, cols].reshape(chan, TILE), ((1,), (0,)))
            s = jax.nn.sigmoid(v)
            hb[part, cols] = (v * s).astype(BF)
            sl[part, cols] = s * (1.0 + v * (1.0 - s))
        h = hb[part, :]
        for i, half in enumerate(HALVES):
            cols = pl.ds(*half)
            v = dot(h, W2[:, :, :, cols].reshape(chan, 640), ((1,), (0,)))
            yb[part, cols] = (xr[part, cols].astype(F32) + v).astype(BF)

            @pl.when(seg < SECTIONS - 1)
            def _():
                y_next(m, i).start()

        @pl.when(y_direct(m))
        def _():
            y_skip(m).start()

        return carry

    lax.fori_loop(0, BLOCKS, forward, 0)

    @pl.when(seg == 3)
    def _():
        for m in range(early, BLOCKS):
            y_relay(m).start()

    @pl.when(seg == 0)
    def _():
        for m in range(BLOCKS):
            h_out(m).start()

    @pl.when(seg < 4)
    def _():
        transpose_weights()

    def turn():
        nT[...] = nb[...].T.reshape(nT.shape)
        hT[...] = hb[...].T.reshape(hT.shape)

    @pl.when(seg < 6)
    def _():
        turn()

    def backward(m, carry):
        part = pl.ds(pl.multiple_of(m * step, step), step)

        @pl.when(seg < SECTIONS - 1)
        def _():
            g_next(m).wait_recv()

        @pl.when(seg < 3)
        def _():
            g_skip(m).wait_recv()
            gr[part, :] = (gr[part, :].astype(F32) + gk[part, :].astype(F32)).astype(BF)

        @pl.when(seg == 0)
        def _():
            g_out(m).start()

        g = gr[part, :]
        for j in range(0, chan, TILE):
            cols = pl.ds(j, TILE)
            v = dot(g, T2[:, cols], ((1,), (0,)))
            dz[part, cols] = (v * sl[part, cols]).astype(BF)
        d = dz[part, :]
        for half in HALVES:
            cols = pl.ds(*half)
            dn[:, cols] = dot(d, T1[:, cols], ((1,), (0,)))
        nrm = un[part, :]
        v = dn[...]
        along = jnp.mean(nrm * v, axis=-1, keepdims=True)
        r = rr[part, pl.ds(0, 1)]
        dx[part, :] = (g.astype(F32) + r * (v - nrm * along)).astype(BF)

        @pl.when(seg > 0)
        def _():
            g_next(m).start()

        @pl.when(g_direct(m))
        def _():
            g_skip(m).start()

        return carry

    lax.fori_loop(0, BLOCKS, backward, 0)

    @pl.when(seg == 4)
    def _():
        for m in range(early, BLOCKS):
            g_relay(m).start()

    dx_out = pltpu.make_async_copy(dx, dxo.at[0], lsem.at[6])
    dx_out.start()

    @pl.when(seg >= 6)
    def _():
        turn()

    sunits = [(w, h) for w in (1, 0, 2) for h in range(2)]
    FAR = (2, 1, -1, 0)

    def product(u, i):
        w, h = sunits[u]
        left, right, to = ((nT, dz, G1), (hT, gr, G2), (hU, gz, G3))[w]
        at = offs[axes[h][0]](FAR[i])
        at = (slice(None), at) if h == 0 else (at, slice(None))
        v = dot(left[at[0], at[1]].reshape(320, rows), right[:, pl.ds(*HALVES[h])], ((1,), (0,)))
        to[at[0], at[1], :, pl.ds(*HALVES[h])] = v.astype(BF).reshape(4, 80, 640)

    def block(u, first, second, part=ALL):
        w, h = sunits[u]
        return one((G1, G2, G3)[w], h, offs[axes[h][0]](first), offs[axes[h][1]](second), part)

    def scopy(u, kind, src, dst, leg, way):
        k = u * 16 + kind
        return pltpu.make_async_remote_copy(
            src_ref=src, dst_ref=dst, send_sem=ssend.at[k], recv_sem=srecv.at[k],
            device_id=dev(axes[sunits[u][1]][leg], way),
        )

    def out_way(i):
        return 1 if i < 2 else -1

    def opposite(u, i):
        return scopy(u, i, block(u, FAR[i], 2), r1.at[u, i], 1, out_way(i))

    def beside(u, i, way):
        k = 4 + 2 * i + (way < 0)
        return scopy(u, k, block(u, FAR[i], way), r2.at[u, i, int(way < 0)], 1, way)

    def last_opposite(u, way):
        part = share(u, way)
        return scopy(u, 12 + (way < 0), block(u, 2, 0, part), r4.at[u, part], 0, way)

    def last_beside(u, way):
        return scopy(u, 14 + (way < 0), block(u, way, 0), r5.at[u, int(way < 0)], 0, way)

    def add(ref, *values):
        total = ref[...].astype(F32)
        for value in values:
            total = total + value.astype(F32)
        ref[...] = total.astype(BF)

    def leave(u, i):
        product(u, i)
        opposite(u, i).start()
        beside(u, i, -out_way(i)).start()

    def go_beside(u, i):
        way = out_way(i)
        opposite(u, i).wait_recv()
        add(block(u, FAR[i], way), r1[u, i])
        beside(u, i, way).start()

    def arrive(u, i):
        beside(u, i, 1).wait_recv()
        beside(u, i, -1).wait_recv()
        if i < 3:
            add(block(u, FAR[i], 0), r2[u, i, 0], r2[u, i, 1])
        if i == 0:
            last_opposite(u, 1).start()
            last_opposite(u, -1).start()
        elif i < 3:
            way = FAR[i]
            part = share(u, way)
            last_opposite(u, way).wait_recv()
            add(block(u, way, 0, part), r4[u, part])
            last_beside(u, way).start()
        else:
            last_beside(u, 1).wait_recv()
            last_beside(u, -1).wait_recv()
            w, h = sunits[u]
            total = block(u, 0, 0)[...].astype(F32)
            for value in (r2[u, i, 0], r2[u, i, 1], r5[u, 0], r5[u, 1]):
                total = total + value.astype(F32)
            to = (fg.at[0], sg.at[0], accb)[w]
            to[:, pl.ds(*HALVES[h])] = total.astype(to.dtype)

    def ours(u, do):
        if u < 2:
            pl.when(seg != 0)(do)
        else:
            do()

    def group(units, *steps):
        for u in units:
            ours(u, lambda: [step(u, i) for step, i in steps] and None)

    def result(h):
        part = pl.ds(*HALVES[h])
        return pltpu.make_async_remote_copy(
            src_ref=accb.at[:, part], dst_ref=accr.at[:, part],
            send_sem=ssend.at[96 + h], recv_sem=srecv.at[96 + h],
            device_id={"segment": lax.rem(seg + SECTIONS - HELPER, SECTIONS)},
        )

    def helper(do):
        pl.when(seg == HELPER)(do)

    def take_over():
        for m in range(BLOCKS):
            h_out(m).wait_recv()
            g_out(m).wait_recv()
        hU[...] = hz[...].T.reshape(hU.shape)
        group(more, (leave, 0), (leave, 2))
        group(more, (leave, 1), (leave, 3))

    def give_back():
        group(more, (go_beside, 1), (go_beside, 3))
        for i in (2, 1, 3):
            group(more, (arrive, i))
        result(0).start()
        result(1).start()

    own, more = range(4), range(4, 6)
    group(own, (leave, 0))
    group(own, (leave, 2))
    group(own, (go_beside, 0))
    group(own, (leave, 1))
    group(own, (go_beside, 2))
    group(own, (arrive, 0))
    group(own, (leave, 3))
    group(own, (go_beside, 1))
    group(own, (arrive, 2))
    group(own, (go_beside, 3))
    group(own, (arrive, 1))
    helper(take_over)
    helper(lambda: group(more, (go_beside, 0), (go_beside, 2), (arrive, 0)))
    helper(give_back)
    group(own, (arrive, 3))

    @pl.when(seg == 0)
    def _():
        for h in range(2):
            result(h).wait_recv()
        sg[0] = accr[...].astype(F32)

    def scattered(u):
        for k in range(4):
            opposite(u, k).wait_send()
            beside(u, k, 1).wait_send()
            beside(u, k, -1).wait_send()
        for way in (1, -1):
            last_opposite(u, way).wait_send()
            last_beside(u, way).wait_send()

    def gathered(u):
        for k in range(4):
            first_leg(u, k).wait_send()
            second_leg(u, k, 1).wait_send()
            second_leg(u, k, -1).wait_send()
            second_on(u, k).wait_send()

    each(gathered)
    for u in range(4):
        ours(u, lambda: scattered(u))

    @pl.when(seg == 1)
    def _():
        hand(0, 0).wait_send()

    @pl.when(seg == HELPER)
    def _():
        gathered(4)
        for k in range(1, 16):
            hand(k // 4, k % 4).wait_send()

    @pl.when(seg == HELPER)
    def _():
        for h in range(2):
            scattered(4 + h)
            result(h).wait_send()

    @pl.when(seg == 0)
    def _():
        for m in range(BLOCKS):
            h_out(m).wait_send()
            g_out(m).wait_send()

    @pl.when(seg == 3)
    def _():
        for m in range(early, BLOCKS):
            y_relay(m).wait_send()

    @pl.when(seg == 4)
    def _():
        for m in range(early, BLOCKS):
            g_relay(m).wait_send()

    def sent(m, carry):
        @pl.when(seg < SECTIONS - 1)
        def _():
            y_next(m, 0).wait_send()
            y_next(m, 1).wait_send()

        @pl.when(y_direct(m))
        def _():
            y_skip(m).wait_send()

        @pl.when(seg > 0)
        def _():
            g_next(m).wait_send()

        @pl.when(g_direct(m))
        def _():
            g_skip(m).wait_send()

        return carry

    lax.fori_loop(0, BLOCKS, sent, 0)
    dx_out.wait()


def local(tokens, grad_out, first_weight, second_weight, emb_table, level_scale, timesteps, levels):
    rows, chan = tokens.shape
    depth = first_weight.shape[1]
    step = rows // BLOCKS
    samples = timesteps.shape[0]
    full = (RING, RING, depth, chan)
    vm = pltpu.VMEM
    dma = pltpu.SemaphoreType.DMA
    act = vm((rows, chan), BF)
    act32 = vm((rows, chan), F32)
    anyspec = pl.BlockSpec(memory_space=pl.ANY)
    vmspec = pl.BlockSpec(memory_space=pltpu.VMEM)
    smem = pl.BlockSpec(memory_space=pltpu.SMEM)
    macs = 6 * rows * chan * chan
    return pl.pallas_call(
        kernel,
        out_shape=(
            vm((1, depth, chan), F32),
            vm((1, depth, chan), F32),
            vm((1, rows, chan), BF),
        ),
        in_specs=[anyspec] * 6 + [smem] * 2,
        out_specs=(vmspec,) * 3,
        scratch_shapes=[
            vm(full, BF), vm(full, BF), vm((chan, chan), BF), vm((chan, chan), BF),
            vm(full, BF), vm(full, BF),
            vm((RING, RING, depth, rows), BF), vm((RING, RING, depth, rows), BF),
            act, act, act, act, act, act32, act32, act, act, act,
            vm((step, chan), F32), act, vm((rows, 128), F32), vm((samples, chan), F32),
            act, act, vm((RING, RING, depth, rows), BF), vm(full, BF),
            vm((depth, chan), BF), vm((depth, chan), BF), vm((RING, RING, depth, 640), BF),
            vm(emb_table.shape, F32), vm(level_scale.shape, F32),
            vm((6, 4, depth, 640), BF), vm((6, 4, 2, depth, 640), BF),
            vm((6, depth, 640), BF), vm((6, 2, depth, 640), BF),
            dma((96,)), dma((96,)), dma((100,)), dma((100,)),
            dma((7 * BLOCKS,)), dma((7 * BLOCKS,)), dma((7,)), pltpu.SemaphoreType.REGULAR,
        ],
        compiler_params=pltpu.CompilerParams(
            collective_id=0, has_side_effects=True, vmem_limit_bytes=60 * 1024 * 1024
        ),
        cost_estimate=pl.CostEstimate(
            flops=2 * macs, bytes_accessed=16 * 1024 * 1024, transcendentals=rows * chan
        ),
        name="sections",
    )(tokens, grad_out, first_weight, second_weight, emb_table, level_scale, timesteps, levels)


def solution(mesh):
    weights = P("segment", "dp", None)
    in_specs = (P("dp", None), P("dp", None), weights, weights, P(), P(), P("dp"), P("segment"))
    out_specs = (weights, weights, weights)
    return jax.shard_map(local, mesh=mesh, in_specs=in_specs, out_specs=out_specs, check_vma=False)
```

```python
import functools

import jax
import jax.numpy as jnp
from jax import lax
from jax.experimental import pallas as pl
from jax.experimental.pallas import tpu as pltpu
from jax.sharding import PartitionSpec as P

EPS = 1e-06
SECTIONS = 8
RING = 4
HELPER = 7
BLOCKS = 4
TILE = 128
HALVES = ((0, 640), (640, 640))
F32 = jnp.float32
BF = jnp.bfloat16


def dot(a, b, contract):
    return lax.dot_general(a, b, (contract, ((), ())), preferred_element_type=F32)


def kernel(
    tok, go, w1, w2, emb, lvl, ts, lv,
    fg, sg, dxo,
    W1, W2, T1, T2, G1, G2, nT, hT,
    xr, sk, yb, nb, hb, un, sl, gr, gk, dz, dn, dx, rr, cond,
    hz, gz, hU, G3, accb, accr, part2,
    embv, lvlv, r1, r2, r4, r5,
    gsend, grecv, ssend, srecv, psend, precv, lsem, turn_sem,
):
    seg = lax.axis_index("segment")
    dp = lax.axis_index("dp")
    z, x = dp // RING, dp % RING
    rows, chan = xr.shape
    step = rows // BLOCKS
    samples = ts.shape[0]

    def at_z(i):
        return lax.rem(z + i + RING, RING)

    def at_x(i):
        return lax.rem(x + i + RING, RING)

    def dev(axis, i):
        return {"dp": at_z(i) * RING + x} if axis == "z" else {"dp": z * RING + at_x(i)}

    own1 = pltpu.make_async_copy(w1.at[0], W1.at[z, x], lsem.at[0])
    own2 = pltpu.make_async_copy(w2.at[0], W2.at[z, x], lsem.at[1])
    table = pltpu.make_async_copy(emb, embv, lsem.at[2])
    scales = pltpu.make_async_copy(lvl, lvlv, lsem.at[3])
    own1.start()
    own2.start()
    table.start()
    scales.start()
    tok_in = pltpu.make_async_copy(tok, xr, lsem.at[4])
    go_in = pltpu.make_async_copy(go, gr, lsem.at[5])

    @pl.when(seg == 0)
    def _():
        tok_in.start()

    @pl.when(seg == SECTIONS - 1)
    def _():
        go_in.start()

    barrier = pltpu.get_barrier_semaphore()
    for axis in ("z", "x"):
        for way in (1, -1):
            pl.semaphore_signal(barrier, inc=1, device_id=dev(axis, way))

    @pl.when(seg > 0)
    def _():
        pl.semaphore_signal(barrier, inc=1, device_id={"segment": seg - 1})

    @pl.when(seg < SECTIONS - 1)
    def _():
        pl.semaphore_signal(barrier, inc=1, device_id={"segment": seg + 1})

    relay = jnp.logical_and(seg > 1, seg < 6)

    @pl.when(relay)
    def _():
        pl.semaphore_signal(barrier, inc=1, device_id={"segment": jnp.where(seg < 4, seg + 2, seg - 2)})

    helped = jnp.logical_or(seg == 1, seg == HELPER)

    @pl.when(helped)
    def _():
        pl.semaphore_signal(barrier, inc=1, device_id={"segment": 1 + HELPER - seg})

    far = jnp.logical_or(seg < 3, seg > 4)

    @pl.when(far)
    def _():
        pl.semaphore_signal(barrier, inc=1, device_id={"segment": SECTIONS - 1 - seg})

    pl.semaphore_wait(
        barrier,
        4
        + (seg > 0).astype(jnp.int32)
        + (seg < SECTIONS - 1).astype(jnp.int32)
        + far.astype(jnp.int32)
        + relay.astype(jnp.int32)
        + helped.astype(jnp.int32),
    )
    own1.wait()
    own2.wait()

    units = [(w, h) for w in range(2) for h in range(2)] + [(2, 1)]
    axes = (("x", "z"), ("z", "x"))
    offs = {"x": at_x, "z": at_z}
    ALL, TOP, LOW = pl.ds(0, 80), pl.ds(0, 48), pl.ds(48, 32)

    def one(ref, h, first, second, part=ALL):
        i = (second, first) if h == 0 else (first, second)
        return ref.at[i[0], i[1], part, pl.ds(*HALVES[h])]

    def gcopy(u, kind, first, second, part, leg, way):
        w, h = units[u]
        at = (offs[axes[h][0]](first), offs[axes[h][1]](second))
        if w == 2:
            ref = part2.at[at[0], at[1], part]
        else:
            ref = one((W1, W2)[w], h, *at, part)
        k = u * 16 + kind
        return pltpu.make_async_remote_copy(
            src_ref=ref, dst_ref=ref, send_sem=gsend.at[k], recv_sem=grecv.at[k],
            device_id=dev(axes[h][leg], way),
        )

    NEAR = (0, -1, 1, 2)

    def share(u, way):
        return TOP if (way > 0) == (u % 4 < 2) else LOW

    def first_leg(u, kind):
        return gcopy(
            u, kind, (0, 0, -1, 1)[kind], 0, (ALL, ALL, share(u, 1), share(u, -1))[kind], 0, (1, -1, 1, -1)[kind]
        )

    def second_leg(u, i, way):
        return gcopy(u, 4 + 2 * i + (way < 0), NEAR[i], 0, ALL, 1, way)

    def second_on(u, i):
        way = 1 if i < 2 else -1
        return gcopy(u, 12 + i, NEAR[i], -way, ALL, 1, way)

    def spread(u, i):
        second_leg(u, i, 1).start()
        second_leg(u, i, -1).start()

    def pass_on(u, i):
        second_leg(u, i, 1 if i < 2 else -1).wait_recv()
        second_on(u, i).start()

    PLACES = (0, -1, 1, 2)

    def hand(i, j):
        at = (at_z(NEAR[i]), at_x(PLACES[j]))
        there = W2.at[at[0], at[1], :, pl.ds(*HALVES[1])]
        src, dst, to = (part2.at[at[0], at[1]], there, 1) if i + j else (there, part2.at[z, x], HELPER)
        k = 80 + 4 * i + j
        return pltpu.make_async_remote_copy(
            src_ref=src, dst_ref=dst, send_sem=gsend.at[k], recv_sem=grecv.at[k],
            device_id={"segment": to},
        )

    def gather_for_another():
        hand(0, 0).wait_recv()
        first_leg(4, 0).start()
        first_leg(4, 1).start()
        spread(4, 0)
        first_leg(4, 0).wait_recv()
        first_leg(4, 2).start()
        first_leg(4, 1).wait_recv()
        first_leg(4, 3).start()
        spread(4, 1)
        spread(4, 2)
        hand(1, 0).start()
        hand(2, 0).start()
        pass_on(4, 0)
        hand(0, 1).start()
        first_leg(4, 2).wait_recv()
        first_leg(4, 3).wait_recv()
        spread(4, 3)
        hand(3, 0).start()
        for i in range(1, 4):
            pass_on(4, i)
            hand(i, 1 if i < 2 else 2).start()
        for i in range(4):
            second_leg(4, i, -1 if i < 2 else 1).wait_recv()
            hand(i, 2 if i < 2 else 1).start()
            second_on(4, i).wait_recv()
            hand(i, 3).start()

    @pl.when(seg == 1)
    def _():
        hand(0, 0).start()

    @pl.when(seg == HELPER)
    def _():
        gather_for_another()

    odd = lax.rem(seg, 2) == 1

    @pl.when(odd)
    def _():
        pl.semaphore_wait(turn_sem, 1)

    def each(do):
        for u in range(4):
            if u == 3:
                pl.when(seg != 1)(lambda: do(3))
            else:
                do(u)

    def begin(u):
        first_leg(u, 0).start()
        first_leg(u, 1).start()

    def onward(u):
        first_leg(u, 0).wait_recv()
        first_leg(u, 2).start()
        first_leg(u, 1).wait_recv()
        first_leg(u, 3).start()
        spread(u, 1)
        spread(u, 2)

    def across(u):
        pass_on(u, 0)
        first_leg(u, 2).wait_recv()
        first_leg(u, 3).wait_recv()
        spread(u, 3)

    def whole(u):
        for i in range(4):
            second_leg(u, i, -1 if i < 2 else 1).wait_recv()
            second_on(u, i).wait_recv()

    each(begin)
    each(lambda u: spread(u, 0))
    each(onward)
    @pl.when(jnp.logical_not(odd))
    def _():
        pl.semaphore_signal(turn_sem, inc=1, device_id={"segment": lax.rem(seg + 1, SECTIONS)})

    each(across)

    for i in range(1, 4):
        each(lambda u: pass_on(u, i))

    table.wait()
    scales.wait()
    scale_row = lvlv[pl.ds(lv[0], 1), :]
    for i in range(samples):
        cond[pl.ds(i, 1), :] = embv[pl.ds(ts[i], 1), :] * scale_row

    @pl.when(seg == 0)
    def _():
        tok_in.wait()

    @pl.when(seg == SECTIONS - 1)
    def _():
        go_in.wait()

    each(whole)

    @pl.when(seg == 1)
    def _():
        for k in range(1, 16):
            hand(k // 4, k % 4).wait_recv()

    def transpose_weights():
        for j in range(0, chan, 256):
            T1[pl.ds(j, 256), :] = W1[:, :, :, pl.ds(j, 256)].reshape(chan, 256).T
            T2[pl.ds(j, 256), :] = W2[:, :, :, pl.ds(j, 256)].reshape(chan, 256).T

    @pl.when(seg >= 4)
    def _():
        transpose_weights()

    def pcopy(kind, m, src, dst, to, cols=(0, 1280)):
        k = kind * BLOCKS + m
        part = pl.ds(pl.multiple_of(m * step, step), step)
        return pltpu.make_async_remote_copy(
            src_ref=src.at[part, pl.ds(*cols)], dst_ref=dst.at[part, pl.ds(*cols)],
            send_sem=psend.at[k], recv_sem=precv.at[k], device_id={"segment": to},
        )

    def y_next(m, i):
        return pcopy((0, 6)[i], m, yb, xr, lax.rem(seg + 1, SECTIONS), HALVES[i])

    def y_skip(m):
        return pcopy(1, m, yb, sk, SECTIONS - 1 - seg)

    def g_next(m):
        return pcopy(2, m, dx, gr, lax.rem(seg + SECTIONS - 1, SECTIONS))

    def g_skip(m):
        return pcopy(3, m, dx, gk, SECTIONS - 1 - seg)

    def y_relay(m):
        return pcopy(1, m, xr, sk, lax.rem(seg + 2, SECTIONS))

    def g_relay(m):
        return pcopy(3, m, gr, gk, lax.rem(seg + SECTIONS - 2, SECTIONS))

    def h_out(m):
        return pcopy(4, m, hb, hz, HELPER)

    def g_out(m):
        return pcopy(5, m, gr, gz, HELPER)

    early = BLOCKS // 2

    def y_direct(m):
        return jnp.logical_or(seg < 2, jnp.logical_and(seg == 2, m < early))

    def g_direct(m):
        return jnp.logical_or(seg > 5, jnp.logical_and(seg == 5, m < early))

    def forward(m, carry):
        part = pl.ds(pl.multiple_of(m * step, step), step)

        @pl.when(seg > 0)
        def _():
            y_next(m, 0).wait_recv()
            y_next(m, 1).wait_recv()

        @pl.when(seg > 4)
        def _():
            y_skip(m).wait_recv()
            xr[part, :] = (xr[part, :].astype(F32) + sk[part, :].astype(F32)).astype(BF)

        row = cond[pl.ds(m // (BLOCKS // samples), 1), :]
        u = xr[part, :].astype(F32) + row
        r = lax.rsqrt(jnp.mean(u * u, axis=-1, keepdims=True) + EPS)
        un[part, :] = u * r
        rr[part, :] = jnp.broadcast_to(r, (step, 128))
        n = (u * r).astype(BF)
        nb[part, :] = n
        for j in range(0, chan, TILE):
            cols = pl.ds(j, TILE)
            v = dot(n, W1[:, :, :, cols].reshape(chan, TILE), ((1,), (0,)))
            s = jax.nn.sigmoid(v)
            hb[part, cols] = (v * s).astype(BF)
            sl[part, cols] = s * (1.0 + v * (1.0 - s))
        h = hb[part, :]
        for i, half in enumerate(HALVES):
            cols = pl.ds(*half)
            v = dot(h, W2[:, :, :, cols].reshape(chan, 640), ((1,), (0,)))
            yb[part, cols] = (xr[part, cols].astype(F32) + v).astype(BF)

            @pl.when(seg < SECTIONS - 1)
            def _():
                y_next(m, i).start()

        @pl.when(y_direct(m))
        def _():
            y_skip(m).start()

        return carry

    lax.fori_loop(0, BLOCKS, forward, 0)

    @pl.when(seg == 3)
    def _():
        for m in range(early, BLOCKS):
            y_relay(m).start()

    @pl.when(seg == 0)
    def _():
        for m in range(BLOCKS):
            h_out(m).start()

    @pl.when(seg < 4)
    def _():
        transpose_weights()

    def turn():
        nT[...] = nb[...].T.reshape(nT.shape)
        hT[...] = hb[...].T.reshape(hT.shape)

    @pl.when(seg < 6)
    def _():
        turn()

    def backward(m, carry):
        part = pl.ds(pl.multiple_of(m * step, step), step)

        @pl.when(seg < SECTIONS - 1)
        def _():
            g_next(m).wait_recv()

        @pl.when(seg < 3)
        def _():
            g_skip(m).wait_recv()
            gr[part, :] = (gr[part, :].astype(F32) + gk[part, :].astype(F32)).astype(BF)

        @pl.when(seg == 0)
        def _():
            g_out(m).start()

        g = gr[part, :]
        for j in range(0, chan, TILE):
            cols = pl.ds(j, TILE)
            v = dot(g, T2[:, cols], ((1,), (0,)))
            dz[part, cols] = (v * sl[part, cols]).astype(BF)
        d = dz[part, :]
        for half in HALVES:
            cols = pl.ds(*half)
            dn[:, cols] = dot(d, T1[:, cols], ((1,), (0,)))
        nrm = un[part, :]
        v = dn[...]
        along = jnp.mean(nrm * v, axis=-1, keepdims=True)
        r = rr[part, pl.ds(0, 1)]
        dx[part, :] = (g.astype(F32) + r * (v - nrm * along)).astype(BF)

        @pl.when(seg > 0)
        def _():
            g_next(m).start()

        @pl.when(g_direct(m))
        def _():
            g_skip(m).start()

        return carry

    lax.fori_loop(0, BLOCKS, backward, 0)

    @pl.when(seg == 4)
    def _():
        for m in range(early, BLOCKS):
            g_relay(m).start()

    dx_out = pltpu.make_async_copy(dx, dxo.at[0], lsem.at[6])
    dx_out.start()

    @pl.when(seg >= 6)
    def _():
        turn()

    sunits = [(w, h) for w in (1, 0, 2) for h in range(2)]
    FAR = (2, 1, -1, 0)

    def product(u, i):
        w, h = sunits[u]
        left, right, to = ((nT, dz, G1), (hT, gr, G2), (hU, gz, G3))[w]
        at = offs[axes[h][0]](FAR[i])
        at = (slice(None), at) if h == 0 else (at, slice(None))
        v = dot(left[at[0], at[1]].reshape(320, rows), right[:, pl.ds(*HALVES[h])], ((1,), (0,)))
        to[at[0], at[1], :, pl.ds(*HALVES[h])] = v.astype(BF).reshape(4, 80, 640)

    def block(u, first, second, part=ALL):
        w, h = sunits[u]
        return one((G1, G2, G3)[w], h, offs[axes[h][0]](first), offs[axes[h][1]](second), part)

    def scopy(u, kind, src, dst, leg, way):
        k = u * 16 + kind
        return pltpu.make_async_remote_copy(
            src_ref=src, dst_ref=dst, send_sem=ssend.at[k], recv_sem=srecv.at[k],
            device_id=dev(axes[sunits[u][1]][leg], way),
        )

    def out_way(i):
        return 1 if i < 2 else -1

    def opposite(u, i):
        return scopy(u, i, block(u, FAR[i], 2), r1.at[u, i], 1, out_way(i))

    def beside(u, i, way):
        k = 4 + 2 * i + (way < 0)
        return scopy(u, k, block(u, FAR[i], way), r2.at[u, i, int(way < 0)], 1, way)

    def last_opposite(u, way):
        part = share(u, way)
        return scopy(u, 12 + (way < 0), block(u, 2, 0, part), r4.at[u, part], 0, way)

    def last_beside(u, way):
        return scopy(u, 14 + (way < 0), block(u, way, 0), r5.at[u, int(way < 0)], 0, way)

    def add(ref, *values):
        total = ref[...].astype(F32)
        for value in values:
            total = total + value.astype(F32)
        ref[...] = total.astype(BF)

    def leave(u, i):
        product(u, i)
        opposite(u, i).start()
        beside(u, i, -out_way(i)).start()

    def go_beside(u, i):
        way = out_way(i)
        opposite(u, i).wait_recv()
        add(block(u, FAR[i], way), r1[u, i])
        beside(u, i, way).start()

    def arrive(u, i):
        beside(u, i, 1).wait_recv()
        beside(u, i, -1).wait_recv()
        if i < 3:
            add(block(u, FAR[i], 0), r2[u, i, 0], r2[u, i, 1])
        if i == 0:
            last_opposite(u, 1).start()
            last_opposite(u, -1).start()
        elif i < 3:
            way = FAR[i]
            part = share(u, way)
            last_opposite(u, way).wait_recv()
            add(block(u, way, 0, part), r4[u, part])
            last_beside(u, way).start()
        else:
            last_beside(u, 1).wait_recv()
            last_beside(u, -1).wait_recv()
            w, h = sunits[u]
            total = block(u, 0, 0)[...].astype(F32)
            for value in (r2[u, i, 0], r2[u, i, 1], r5[u, 0], r5[u, 1]):
                total = total + value.astype(F32)
            to = (fg.at[0], sg.at[0], accb)[w]
            to[:, pl.ds(*HALVES[h])] = total.astype(to.dtype)

    def ours(u, do):
        if u < 2:
            pl.when(seg != 0)(do)
        else:
            do()

    def group(units, *steps):
        for u in units:
            ours(u, lambda: [step(u, i) for step, i in steps] and None)

    def result(h):
        part = pl.ds(*HALVES[h])
        return pltpu.make_async_remote_copy(
            src_ref=accb.at[:, part], dst_ref=accr.at[:, part],
            send_sem=ssend.at[96 + h], recv_sem=srecv.at[96 + h],
            device_id={"segment": lax.rem(seg + SECTIONS - HELPER, SECTIONS)},
        )

    def helper(do):
        pl.when(seg == HELPER)(do)

    def take_over():
        for m in range(BLOCKS):
            h_out(m).wait_recv()
            g_out(m).wait_recv()
        hU[...] = hz[...].T.reshape(hU.shape)
        group(more, (leave, 0), (leave, 2))
        group(more, (go_beside, 0), (go_beside, 2))
        group(more, (leave, 1), (leave, 3))
        group(more, (arrive, 0))

    def give_back():
        group(more, (go_beside, 1), (go_beside, 3))
        group(more, (arrive, 2))
        group(more, (arrive, 1))
        for h in range(2):
            arrive(4 + h, 3)
            result(h).start()

    own, more = range(4), range(4, 6)
    group(own, (leave, 0))
    group(own, (leave, 2))
    group(own, (go_beside, 0))
    group(own, (leave, 1))
    group(own, (go_beside, 2))
    group(own, (arrive, 0))
    group(own, (leave, 3))
    group(own, (go_beside, 1))
    group(own, (arrive, 2))
    group(own, (go_beside, 3))
    group(own, (arrive, 1))
    helper(take_over)
    helper(give_back)
    group(own, (arrive, 3))

    @pl.when(seg == 0)
    def _():
        for h in range(2):
            result(h).wait_recv()
        sg[0] = accr[...].astype(F32)

    def scattered(u):
        for k in range(4):
            opposite(u, k).wait_send()
            beside(u, k, 1).wait_send()
            beside(u, k, -1).wait_send()
        for way in (1, -1):
            last_opposite(u, way).wait_send()
            last_beside(u, way).wait_send()

    def gathered(u):
        for k in range(4):
            first_leg(u, k).wait_send()
            second_leg(u, k, 1).wait_send()
            second_leg(u, k, -1).wait_send()
            second_on(u, k).wait_send()

    each(gathered)
    for u in range(4):
        ours(u, lambda: scattered(u))

    @pl.when(seg == 1)
    def _():
        hand(0, 0).wait_send()

    @pl.when(seg == HELPER)
    def _():
        gathered(4)
        for k in range(1, 16):
            hand(k // 4, k % 4).wait_send()

    @pl.when(seg == HELPER)
    def _():
        for h in range(2):
            scattered(4 + h)
            result(h).wait_send()

    @pl.when(seg == 0)
    def _():
        for m in range(BLOCKS):
            h_out(m).wait_send()
            g_out(m).wait_send()

    @pl.when(seg == 3)
    def _():
        for m in range(early, BLOCKS):
            y_relay(m).wait_send()

    @pl.when(seg == 4)
    def _():
        for m in range(early, BLOCKS):
            g_relay(m).wait_send()

    def sent(m, carry):
        @pl.when(seg < SECTIONS - 1)
        def _():
            y_next(m, 0).wait_send()
            y_next(m, 1).wait_send()

        @pl.when(y_direct(m))
        def _():
            y_skip(m).wait_send()

        @pl.when(seg > 0)
        def _():
            g_next(m).wait_send()

        @pl.when(g_direct(m))
        def _():
            g_skip(m).wait_send()

        return carry

    lax.fori_loop(0, BLOCKS, sent, 0)
    dx_out.wait()


def local(tokens, grad_out, first_weight, second_weight, emb_table, level_scale, timesteps, levels):
    rows, chan = tokens.shape
    depth = first_weight.shape[1]
    step = rows // BLOCKS
    samples = timesteps.shape[0]
    full = (RING, RING, depth, chan)
    vm = pltpu.VMEM
    dma = pltpu.SemaphoreType.DMA
    act = vm((rows, chan), BF)
    act32 = vm((rows, chan), F32)
    anyspec = pl.BlockSpec(memory_space=pl.ANY)
    vmspec = pl.BlockSpec(memory_space=pltpu.VMEM)
    smem = pl.BlockSpec(memory_space=pltpu.SMEM)
    macs = 6 * rows * chan * chan
    return pl.pallas_call(
        kernel,
        out_shape=(
            vm((1, depth, chan), F32),
            vm((1, depth, chan), F32),
            vm((1, rows, chan), BF),
        ),
        in_specs=[anyspec] * 6 + [smem] * 2,
        out_specs=(vmspec,) * 3,
        scratch_shapes=[
            vm(full, BF), vm(full, BF), vm((chan, chan), BF), vm((chan, chan), BF),
            vm(full, BF), vm(full, BF),
            vm((RING, RING, depth, rows), BF), vm((RING, RING, depth, rows), BF),
            act, act, act, act, act, act32, act32, act, act, act,
            vm((step, chan), F32), act, vm((rows, 128), F32), vm((samples, chan), F32),
            act, act, vm((RING, RING, depth, rows), BF), vm(full, BF),
            vm((depth, chan), BF), vm((depth, chan), BF), vm((RING, RING, depth, 640), BF),
            vm(emb_table.shape, F32), vm(level_scale.shape, F32),
            vm((6, 4, depth, 640), BF), vm((6, 4, 2, depth, 640), BF),
            vm((6, depth, 640), BF), vm((6, 2, depth, 640), BF),
            dma((96,)), dma((96,)), dma((100,)), dma((100,)),
            dma((7 * BLOCKS,)), dma((7 * BLOCKS,)), dma((7,)), pltpu.SemaphoreType.REGULAR,
        ],
        compiler_params=pltpu.CompilerParams(
            collective_id=0, has_side_effects=True, vmem_limit_bytes=60 * 1024 * 1024
        ),
        cost_estimate=pl.CostEstimate(
            flops=2 * macs, bytes_accessed=16 * 1024 * 1024, transcendentals=rows * chan
        ),
        name="sections",
    )(tokens, grad_out, first_weight, second_weight, emb_table, level_scale, timesteps, levels)


def solution(mesh):
    weights = P("segment", "dp", None)
    in_specs = (P("dp", None), P("dp", None), weights, weights, P(), P(), P("dp"), P("segment"))
    out_specs = (weights, weights, weights)
    return jax.shard_map(local, mesh=mesh, in_specs=in_specs, out_specs=out_specs, check_vma=False)
```

```python
import functools

import jax
import jax.numpy as jnp
from jax import lax
from jax.experimental import pallas as pl
from jax.experimental.pallas import tpu as pltpu
from jax.sharding import PartitionSpec as P

EPS = 1e-06
SECTIONS = 8
RING = 4
HELPER = 7
BLOCKS = 4
TILE = 128
HALVES = ((0, 640), (640, 640))
F32 = jnp.float32
BF = jnp.bfloat16


def dot(a, b, contract):
    return lax.dot_general(a, b, (contract, ((), ())), preferred_element_type=F32)


def kernel(
    tok, go, w1, w2, emb, lvl, ts, lv,
    fg, sg, dxo,
    W1, W2, T1, T2, G1, G2, nT, hT,
    xr, sk, yb, nb, hb, un, sl, zb, gr, gk, dz, dx, rr, cond,
    hz, gz, hU, G3, accb, accr, part2,
    embv, lvlv, r1, r2, r4, r5,
    gsend, grecv, ssend, srecv, psend, precv, lsem, turn_sem,
):
    seg = lax.axis_index("segment")
    dp = lax.axis_index("dp")
    z, x = dp // RING, dp % RING
    rows, chan = xr.shape
    step = rows // BLOCKS
    samples = ts.shape[0]

    def at_z(i):
        return lax.rem(z + i + RING, RING)

    def at_x(i):
        return lax.rem(x + i + RING, RING)

    def dev(axis, i):
        return {"dp": at_z(i) * RING + x} if axis == "z" else {"dp": z * RING + at_x(i)}

    own1 = pltpu.make_async_copy(w1.at[0], W1.at[z, x], lsem.at[0])
    own2 = pltpu.make_async_copy(w2.at[0], W2.at[z, x], lsem.at[1])
    table = pltpu.make_async_copy(emb, embv, lsem.at[2])
    scales = pltpu.make_async_copy(lvl, lvlv, lsem.at[3])
    own1.start()
    own2.start()
    table.start()
    scales.start()
    tok_in = pltpu.make_async_copy(tok, xr, lsem.at[4])
    go_in = pltpu.make_async_copy(go, gr, lsem.at[5])

    @pl.when(seg == 0)
    def _():
        tok_in.start()

    @pl.when(seg == SECTIONS - 1)
    def _():
        go_in.start()

    barrier = pltpu.get_barrier_semaphore()
    for axis in ("z", "x"):
        for way in (1, -1):
            pl.semaphore_signal(barrier, inc=1, device_id=dev(axis, way))

    @pl.when(seg > 0)
    def _():
        pl.semaphore_signal(barrier, inc=1, device_id={"segment": seg - 1})

    @pl.when(seg < SECTIONS - 1)
    def _():
        pl.semaphore_signal(barrier, inc=1, device_id={"segment": seg + 1})

    relay = jnp.logical_and(seg > 1, seg < 6)

    @pl.when(relay)
    def _():
        pl.semaphore_signal(barrier, inc=1, device_id={"segment": jnp.where(seg < 4, seg + 2, seg - 2)})

    helped = jnp.logical_or(seg == 1, seg == HELPER)

    @pl.when(helped)
    def _():
        pl.semaphore_signal(barrier, inc=1, device_id={"segment": 1 + HELPER - seg})

    far = jnp.logical_or(seg < 3, seg > 4)

    @pl.when(far)
    def _():
        pl.semaphore_signal(barrier, inc=1, device_id={"segment": SECTIONS - 1 - seg})

    pl.semaphore_wait(
        barrier,
        4
        + (seg > 0).astype(jnp.int32)
        + (seg < SECTIONS - 1).astype(jnp.int32)
        + far.astype(jnp.int32)
        + relay.astype(jnp.int32)
        + helped.astype(jnp.int32),
    )
    own1.wait()
    own2.wait()

    units = [(w, h) for w in range(2) for h in range(2)] + [(2, 1)]
    axes = (("x", "z"), ("z", "x"))
    offs = {"x": at_x, "z": at_z}
    ALL, TOP, LOW = pl.ds(0, 80), pl.ds(0, 48), pl.ds(48, 32)

    def one(ref, h, first, second, part=ALL):
        i = (second, first) if h == 0 else (first, second)
        return ref.at[i[0], i[1], part, pl.ds(*HALVES[h])]

    def gcopy(u, kind, first, second, part, leg, way):
        w, h = units[u]
        at = (offs[axes[h][0]](first), offs[axes[h][1]](second))
        if w == 2:
            ref = part2.at[at[0], at[1], part]
        else:
            ref = one((W1, W2)[w], h, *at, part)
        k = u * 16 + kind
        return pltpu.make_async_remote_copy(
            src_ref=ref, dst_ref=ref, send_sem=gsend.at[k], recv_sem=grecv.at[k],
            device_id=dev(axes[h][leg], way),
        )

    NEAR = (0, -1, 1, 2)

    def share(u, way):
        return TOP if (way > 0) == (u % 4 < 2) else LOW

    def first_leg(u, kind):
        return gcopy(
            u, kind, (0, 0, -1, 1)[kind], 0, (ALL, ALL, share(u, 1), share(u, -1))[kind], 0, (1, -1, 1, -1)[kind]
        )

    def second_leg(u, i, way):
        return gcopy(u, 4 + 2 * i + (way < 0), NEAR[i], 0, ALL, 1, way)

    def second_on(u, i):
        way = 1 if i < 2 else -1
        return gcopy(u, 12 + i, NEAR[i], -way, ALL, 1, way)

    def spread(u, i):
        second_leg(u, i, 1).start()
        second_leg(u, i, -1).start()

    def pass_on(u, i):
        second_leg(u, i, 1 if i < 2 else -1).wait_recv()
        second_on(u, i).start()

    PLACES = (0, -1, 1, 2)

    def hand(i, j):
        at = (at_z(NEAR[i]), at_x(PLACES[j]))
        there = W2.at[at[0], at[1], :, pl.ds(*HALVES[1])]
        src, dst, to = (part2.at[at[0], at[1]], there, 1) if i + j else (there, part2.at[z, x], HELPER)
        k = 80 + 4 * i + j
        return pltpu.make_async_remote_copy(
            src_ref=src, dst_ref=dst, send_sem=gsend.at[k], recv_sem=grecv.at[k],
            device_id={"segment": to},
        )

    def gather_for_another():
        hand(0, 0).wait_recv()
        first_leg(4, 0).start()
        first_leg(4, 1).start()
        spread(4, 0)
        first_leg(4, 0).wait_recv()
        first_leg(4, 2).start()
        first_leg(4, 1).wait_recv()
        first_leg(4, 3).start()
        spread(4, 1)
        spread(4, 2)
        hand(1, 0).start()
        hand(2, 0).start()
        pass_on(4, 0)
        hand(0, 1).start()
        first_leg(4, 2).wait_recv()
        first_leg(4, 3).wait_recv()
        spread(4, 3)
        hand(3, 0).start()
        for i in range(1, 4):
            pass_on(4, i)
            hand(i, 1 if i < 2 else 2).start()
        for i in range(4):
            second_leg(4, i, -1 if i < 2 else 1).wait_recv()
            hand(i, 2 if i < 2 else 1).start()
            second_on(4, i).wait_recv()
            hand(i, 3).start()

    @pl.when(seg == 1)
    def _():
        hand(0, 0).start()

    @pl.when(seg == HELPER)
    def _():
        gather_for_another()

    odd = lax.rem(seg, 2) == 1

    @pl.when(odd)
    def _():
        pl.semaphore_wait(turn_sem, 1)

    def each(do):
        for u in range(4):
            if u == 3:
                pl.when(seg != 1)(lambda: do(3))
            else:
                do(u)

    def begin(u):
        first_leg(u, 0).start()
        first_leg(u, 1).start()

    def onward(u):
        first_leg(u, 0).wait_recv()
        first_leg(u, 2).start()
        first_leg(u, 1).wait_recv()
        first_leg(u, 3).start()
        spread(u, 1)
        spread(u, 2)

    def across(u):
        pass_on(u, 0)
        first_leg(u, 2).wait_recv()
        first_leg(u, 3).wait_recv()
        spread(u, 3)

    def whole(u):
        for i in range(4):
            second_leg(u, i, -1 if i < 2 else 1).wait_recv()
            second_on(u, i).wait_recv()

    each(begin)
    each(lambda u: spread(u, 0))
    each(onward)
    @pl.when(jnp.logical_not(odd))
    def _():
        pl.semaphore_signal(turn_sem, inc=1, device_id={"segment": lax.rem(seg + 1, SECTIONS)})

    each(across)

    each(lambda u: [pass_on(u, i) for i in range(1, 4)] and None)

    table.wait()
    scales.wait()
    scale_row = lvlv[pl.ds(lv[0], 1), :]
    for i in range(samples):
        cond[pl.ds(i, 1), :] = embv[pl.ds(ts[i], 1), :] * scale_row

    @pl.when(seg == 0)
    def _():
        tok_in.wait()

    @pl.when(seg == SECTIONS - 1)
    def _():
        go_in.wait()

    each(whole)

    @pl.when(seg == 1)
    def _():
        for k in range(1, 16):
            hand(k // 4, k % 4).wait_recv()

    def transpose_weights():
        for j in range(0, chan, 256):
            T1[pl.ds(j, 256), :] = W1[:, :, :, pl.ds(j, 256)].reshape(chan, 256).T
            T2[pl.ds(j, 256), :] = W2[:, :, :, pl.ds(j, 256)].reshape(chan, 256).T

    @pl.when(seg >= 4)
    def _():
        transpose_weights()

    def pcopy(kind, m, src, dst, to, cols=(0, 1280)):
        k = kind * BLOCKS + m
        part = pl.ds(pl.multiple_of(m * step, step), step)
        return pltpu.make_async_remote_copy(
            src_ref=src.at[part, pl.ds(*cols)], dst_ref=dst.at[part, pl.ds(*cols)],
            send_sem=psend.at[k], recv_sem=precv.at[k], device_id={"segment": to},
        )

    def y_next(m, i):
        return pcopy((0, 6)[i], m, yb, xr, lax.rem(seg + 1, SECTIONS), HALVES[i])

    def y_skip(m):
        return pcopy(1, m, yb, sk, SECTIONS - 1 - seg)

    def g_next(m, i):
        return pcopy((2, 7)[i], m, dx, gr, lax.rem(seg + SECTIONS - 1, SECTIONS), HALVES[i])

    def g_skip(m):
        return pcopy(3, m, dx, gk, SECTIONS - 1 - seg)

    def y_relay(m):
        return pcopy(1, m, xr, sk, lax.rem(seg + 2, SECTIONS))

    def g_relay(m):
        return pcopy(3, m, gr, gk, lax.rem(seg + SECTIONS - 2, SECTIONS))

    def h_out(m):
        return pcopy(4, m, hb, hz, HELPER)

    def g_out(m):
        return pcopy(5, m, gr, gz, HELPER)

    early = BLOCKS // 2

    def y_direct(m):
        return jnp.logical_or(seg < 2, jnp.logical_and(seg == 2, m < early))

    def g_direct(m):
        return jnp.logical_or(seg > 5, jnp.logical_and(seg == 5, m < early))

    def forward(m, carry):
        part = pl.ds(pl.multiple_of(m * step, step), step)

        @pl.when(seg > 0)
        def _():
            y_next(m, 0).wait_recv()
            y_next(m, 1).wait_recv()

        @pl.when(seg > 4)
        def _():
            y_skip(m).wait_recv()
            xr[part, :] = (xr[part, :].astype(F32) + sk[part, :].astype(F32)).astype(BF)

        row = cond[pl.ds(m // (BLOCKS // samples), 1), :]
        u = xr[part, :].astype(F32) + row
        r = lax.rsqrt(jnp.mean(u * u, axis=-1, keepdims=True) + EPS)
        un[part, :] = u * r
        rr[part, :] = jnp.broadcast_to(r, (step, 128))
        n = (u * r).astype(BF)
        nb[part, :] = n
        for j in range(0, chan, TILE):
            cols = pl.ds(j, TILE)
            v = dot(n, W1[:, :, :, cols].reshape(chan, TILE), ((1,), (0,)))
            s = jax.nn.sigmoid(v)
            zb[part, cols] = v
            hb[part, cols] = (v * s).astype(BF)
            sl[part, cols] = s * (1.0 + v * (1.0 - s))
        h = hb[part, :]
        for i, half in enumerate(HALVES):
            cols = pl.ds(*half)
            v = dot(h, W2[:, :, :, cols].reshape(chan, 640), ((1,), (0,)))
            yb[part, cols] = (xr[part, cols].astype(F32) + v).astype(BF)

            @pl.when(seg < SECTIONS - 1)
            def _():
                y_next(m, i).start()

        @pl.when(y_direct(m))
        def _():
            y_skip(m).start()

        return carry

    lax.fori_loop(0, BLOCKS, forward, 0)

    @pl.when(seg == 3)
    def _():
        for m in range(early, BLOCKS):
            y_relay(m).start()

    @pl.when(seg == 0)
    def _():
        for m in range(BLOCKS):
            h_out(m).start()

    @pl.when(seg < 4)
    def _():
        transpose_weights()

    def turn():
        nT[...] = nb[...].T.reshape(nT.shape)
        hT[...] = hb[...].T.reshape(hT.shape)

    @pl.when(seg < 6)
    def _():
        turn()

    def backward(m, carry):
        part = pl.ds(pl.multiple_of(m * step, step), step)

        @pl.when(seg < SECTIONS - 1)
        def _():
            g_next(m, 0).wait_recv()
            g_next(m, 1).wait_recv()

        @pl.when(seg < 3)
        def _():
            g_skip(m).wait_recv()
            gr[part, :] = (gr[part, :].astype(F32) + gk[part, :].astype(F32)).astype(BF)

        @pl.when(seg == 0)
        def _():
            g_out(m).start()

        g = gr[part, :]
        along = jnp.zeros((step, TILE), F32)
        for j in range(0, chan, TILE):
            cols = pl.ds(j, TILE)
            v = dot(g, T2[:, cols], ((1,), (0,)))
            d = (v * sl[part, cols]).astype(BF)
            dz[part, cols] = d
            along = along + d.astype(F32) * zb[part, cols]
        along = jnp.sum(along, axis=-1, keepdims=True) * (1.0 / chan)
        d = dz[part, :]
        r = rr[part, pl.ds(0, 1)]
        for i, half in enumerate(HALVES):
            cols = pl.ds(*half)
            v = dot(d, T1[:, cols], ((1,), (0,)))
            dx[part, cols] = (gr[part, cols].astype(F32) + r * (v - un[part, cols] * along)).astype(BF)

            @pl.when(seg > 0)
            def _():
                g_next(m, i).start()

        @pl.when(g_direct(m))
        def _():
            g_skip(m).start()

        return carry

    lax.fori_loop(0, BLOCKS, backward, 0)

    @pl.when(seg == 4)
    def _():
        for m in range(early, BLOCKS):
            g_relay(m).start()

    dx_out = pltpu.make_async_copy(dx, dxo.at[0], lsem.at[6])
    dx_out.start()

    @pl.when(seg >= 6)
    def _():
        turn()

    sunits = [(w, h) for w in (1, 0, 2) for h in range(2)]
    FAR = (2, 1, -1, 0)

    def product(u, i):
        w, h = sunits[u]
        left, right, to = ((nT, dz, G1), (hT, gr, G2), (hU, gz, G3))[w]
        at = offs[axes[h][0]](FAR[i])
        at = (slice(None), at) if h == 0 else (at, slice(None))
        v = dot(left[at[0], at[1]].reshape(320, rows), right[:, pl.ds(*HALVES[h])], ((1,), (0,)))
        to[at[0], at[1], :, pl.ds(*HALVES[h])] = v.astype(BF).reshape(4, 80, 640)

    def block(u, first, second, part=ALL):
        w, h = sunits[u]
        return one((G1, G2, G3)[w], h, offs[axes[h][0]](first), offs[axes[h][1]](second), part)

    def scopy(u, kind, src, dst, leg, way):
        k = u * 16 + kind
        return pltpu.make_async_remote_copy(
            src_ref=src, dst_ref=dst, send_sem=ssend.at[k], recv_sem=srecv.at[k],
            device_id=dev(axes[sunits[u][1]][leg], way),
        )

    def out_way(i):
        return 1 if i < 2 else -1

    def opposite(u, i):
        return scopy(u, i, block(u, FAR[i], 2), r1.at[u, i], 1, out_way(i))

    def beside(u, i, way):
        k = 4 + 2 * i + (way < 0)
        return scopy(u, k, block(u, FAR[i], way), r2.at[u, i, int(way < 0)], 1, way)

    def last_opposite(u, way):
        part = share(u, way)
        return scopy(u, 12 + (way < 0), block(u, 2, 0, part), r4.at[u, part], 0, way)

    def last_beside(u, way):
        return scopy(u, 14 + (way < 0), block(u, way, 0), r5.at[u, int(way < 0)], 0, way)

    def add(ref, *values):
        total = ref[...].astype(F32)
        for value in values:
            total = total + value.astype(F32)
        ref[...] = total.astype(BF)

    def leave(u, i):
        product(u, i)
        opposite(u, i).start()
        beside(u, i, -out_way(i)).start()

    def go_beside(u, i):
        way = out_way(i)
        opposite(u, i).wait_recv()
        add(block(u, FAR[i], way), r1[u, i])
        beside(u, i, way).start()

    def arrive(u, i):
        beside(u, i, 1).wait_recv()
        beside(u, i, -1).wait_recv()
        if i < 3:
            add(block(u, FAR[i], 0), r2[u, i, 0], r2[u, i, 1])
        if i == 0:
            last_opposite(u, 1).start()
            last_opposite(u, -1).start()
        elif i < 3:
            way = FAR[i]
            part = share(u, way)
            last_opposite(u, way).wait_recv()
            add(block(u, way, 0, part), r4[u, part])
            last_beside(u, way).start()
        else:
            last_beside(u, 1).wait_recv()
            last_beside(u, -1).wait_recv()
            w, h = sunits[u]
            total = block(u, 0, 0)[...].astype(F32)
            for value in (r2[u, i, 0], r2[u, i, 1], r5[u, 0], r5[u, 1]):
                total = total + value.astype(F32)
            to = (fg.at[0], sg.at[0], accb)[w]
            to[:, pl.ds(*HALVES[h])] = total.astype(to.dtype)

    def ours(u, do):
        if u < 2:
            pl.when(seg != 0)(do)
        else:
            do()

    def group(units, *steps):
        for u in units:
            ours(u, lambda: [step(u, i) for step, i in steps] and None)

    def result(h):
        part = pl.ds(*HALVES[h])
        return pltpu.make_async_remote_copy(
            src_ref=accb.at[:, part], dst_ref=accr.at[:, part],
            send_sem=ssend.at[96 + h], recv_sem=srecv.at[96 + h],
            device_id={"segment": lax.rem(seg + SECTIONS - HELPER, SECTIONS)},
        )

    def helper(do):
        pl.when(seg == HELPER)(do)

    def take_over():
        for m in range(BLOCKS):
            h_out(m).wait_recv()
            g_out(m).wait_recv()
        hU[...] = hz[...].T.reshape(hU.shape)
        group(more, (leave, 0), (leave, 2))
        group(more, (go_beside, 0), (go_beside, 2))
        group(more, (leave, 1), (leave, 3))
        group(more, (arrive, 0))

    def give_back():
        group(more, (go_beside, 1), (go_beside, 3))
        group(more, (arrive, 2))
        group(more, (arrive, 1))
        for h in range(2):
            arrive(4 + h, 3)
            result(h).start()

    own, more = range(4), range(4, 6)
    group(own, (leave, 0))
    group(own, (leave, 2))
    group(own, (go_beside, 0))
    group(own, (go_beside, 2))
    group(own, (leave, 1))
    group(own, (leave, 3))
    group(own, (arrive, 0))
    group(own, (go_beside, 1))
    group(own, (go_beside, 3))
    group(own, (arrive, 2))
    group(own, (arrive, 1))
    helper(take_over)
    helper(give_back)
    group(own, (arrive, 3))

    @pl.when(seg == 0)
    def _():
        for h in range(2):
            result(h).wait_recv()
        sg[0] = accr[...].astype(F32)

    def scattered(u):
        for k in range(4):
            opposite(u, k).wait_send()
            beside(u, k, 1).wait_send()
            beside(u, k, -1).wait_send()
        for way in (1, -1):
            last_opposite(u, way).wait_send()
            last_beside(u, way).wait_send()

    def gathered(u):
        for k in range(4):
            first_leg(u, k).wait_send()
            second_leg(u, k, 1).wait_send()
            second_leg(u, k, -1).wait_send()
            second_on(u, k).wait_send()

    each(gathered)
    for u in range(4):
        ours(u, lambda: scattered(u))

    @pl.when(seg == 1)
    def _():
        hand(0, 0).wait_send()

    @pl.when(seg == HELPER)
    def _():
        gathered(4)
        for k in range(1, 16):
            hand(k // 4, k % 4).wait_send()

    @pl.when(seg == HELPER)
    def _():
        for h in range(2):
            scattered(4 + h)
            result(h).wait_send()

    @pl.when(seg == 0)
    def _():
        for m in range(BLOCKS):
            h_out(m).wait_send()
            g_out(m).wait_send()

    @pl.when(seg == 3)
    def _():
        for m in range(early, BLOCKS):
            y_relay(m).wait_send()

    @pl.when(seg == 4)
    def _():
        for m in range(early, BLOCKS):
            g_relay(m).wait_send()

    def sent(m, carry):
        @pl.when(seg < SECTIONS - 1)
        def _():
            y_next(m, 0).wait_send()
            y_next(m, 1).wait_send()

        @pl.when(y_direct(m))
        def _():
            y_skip(m).wait_send()

        @pl.when(seg > 0)
        def _():
            g_next(m, 0).wait_send()
            g_next(m, 1).wait_send()

        @pl.when(g_direct(m))
        def _():
            g_skip(m).wait_send()

        return carry

    lax.fori_loop(0, BLOCKS, sent, 0)
    dx_out.wait()


def local(tokens, grad_out, first_weight, second_weight, emb_table, level_scale, timesteps, levels):
    rows, chan = tokens.shape
    depth = first_weight.shape[1]
    step = rows // BLOCKS
    samples = timesteps.shape[0]
    full = (RING, RING, depth, chan)
    vm = pltpu.VMEM
    dma = pltpu.SemaphoreType.DMA
    act = vm((rows, chan), BF)
    act32 = vm((rows, chan), F32)
    anyspec = pl.BlockSpec(memory_space=pl.ANY)
    vmspec = pl.BlockSpec(memory_space=pltpu.VMEM)
    smem = pl.BlockSpec(memory_space=pltpu.SMEM)
    macs = 6 * rows * chan * chan
    return pl.pallas_call(
        kernel,
        out_shape=(
            vm((1, depth, chan), F32),
            vm((1, depth, chan), F32),
            vm((1, rows, chan), BF),
        ),
        in_specs=[anyspec] * 6 + [smem] * 2,
        out_specs=(vmspec,) * 3,
        scratch_shapes=[
            vm(full, BF), vm(full, BF), vm((chan, chan), BF), vm((chan, chan), BF),
            vm(full, BF), vm(full, BF),
            vm((RING, RING, depth, rows), BF), vm((RING, RING, depth, rows), BF),
            act, act, act, act, act, act32, act32, act32, act, act, act,
            act, vm((rows, 128), F32), vm((samples, chan), F32),
            act, act, vm((RING, RING, depth, rows), BF), vm(full, BF),
            vm((depth, chan), BF), vm((depth, chan), BF), vm((RING, RING, depth, 640), BF),
            vm(emb_table.shape, F32), vm(level_scale.shape, F32),
            vm((6, 4, depth, 640), BF), vm((6, 4, 2, depth, 640), BF),
            vm((6, depth, 640), BF), vm((6, 2, depth, 640), BF),
            dma((96,)), dma((96,)), dma((100,)), dma((100,)),
            dma((8 * BLOCKS,)), dma((8 * BLOCKS,)), dma((7,)), pltpu.SemaphoreType.REGULAR,
        ],
        compiler_params=pltpu.CompilerParams(
            collective_id=0, has_side_effects=True, vmem_limit_bytes=60 * 1024 * 1024
        ),
        cost_estimate=pl.CostEstimate(
            flops=2 * macs, bytes_accessed=16 * 1024 * 1024, transcendentals=rows * chan
        ),
        name="sections",
    )(tokens, grad_out, first_weight, second_weight, emb_table, level_scale, timesteps, levels)


def solution(mesh):
    weights = P("segment", "dp", None)
    in_specs = (P("dp", None), P("dp", None), weights, weights, P(), P(), P("dp"), P("segment"))
    out_specs = (weights, weights, weights)
    return jax.shard_map(local, mesh=mesh, in_specs=in_specs, out_specs=out_specs, check_vma=False)
```
